128 devices in a mesh: section: 16 (over y, z), mp: 8 (over x, core).
Axes of the slice: x: 4, y: 4, z: 4, core: 2. Of those that a mesh axis runs over, the one named last changes fastest.
Arguments:
- queries: bfloat16 [16384, 4096], P('section', 'mp')
- keys: bfloat16 [2048, 4096], P('section', 'mp')
- values: bfloat16 [2048, 4096], P('section', 'mp'), may hold values from -6 to 6
- out_weight: bfloat16 [4096, 4096], P('mp'), may hold values from -0.09375 to 0.09375
- cotangent: bfloat16 [16384, 4096], P('section', 'mp'), may hold values from -6 to 6
- pack: int32 [16, 1024], P('section'), may hold values from 0 to 2047, as said below
- kv_seg: int32 [16, 1024], P('section'), may hold values from 0 to 3, as said below
- q_seg: int32 [16384], P('section'), may hold values from 0 to 3, as said below
Outputs:
- mixed: bfloat16 [16384, 4096], P('section', 'mp')
- d_queries: bfloat16 [16384, 4096], P('section', 'mp')
- d_keys: float32 [2048, 4096], P('section', 'mp')
- d_values: float32 [2048, 4096], P('section', 'mp')
- d_out_weight: float32 [4096, 4096], P('mp', 'section')
The draws below stay inside these ranges and needn't reach their ends.
Inputs may be any that keep to these rules, and one draw needn't show every extreme that they name: `pack`: the 1024 entries of one row are distinct memory rows. `kv_seg`: along each row the id starts at 0, rises by 0 or 1 from one entry to the next and ends at 3. `q_seg`: the first token of each micro-batch has id 0 and its last token the largest id.
All inputs are finite; a program needn't handle non-finite values.
Results may differ from the reference program's by a relative error of at most 0.0058.
Values may be sent and summed in bfloat16 or wider, within the bound.
No kernel may reach another device: no remote copies, remote signals or barrier semaphores. Data moves between devices by JAX's collectives and lax.ppermute only.
A program may use at most 128 MiB of HBM per device.

```python
import jax
import jax.numpy as jnp
from jax import lax

D = 4096
H = 16
HD = 256
TQ = 1024
KV = 1024
SEG_GAP = 256
MEM = 2048
QROWS = 16384
N_SECTION = 16


def packing_layout(key):
    layout_key = jax.random.fold_in(key, 71)
    perm_key = jax.random.fold_in(layout_key, 1)
    bound_key = jax.random.fold_in(layout_key, 2)
    query_key = jax.random.fold_in(layout_key, 3)
    section_ids = jnp.arange(N_SECTION, dtype=jnp.int32)
    pack = jax.vmap(lambda s: jax.random.permutation(jax.random.fold_in(perm_key, s), MEM)[:KV])(section_ids).astype(jnp.int32)
    seg_count = KV // SEG_GAP
    bounds = jax.vmap(lambda s: jax.random.permutation(jax.random.fold_in(bound_key, s), KV - 1)[:seg_count - 1])(section_ids).astype(jnp.int32) + 1
    positions = jnp.arange(KV, dtype=jnp.int32)
    kv_seg = jnp.sum((positions[None, :, None] >= bounds[:, None, :]).astype(jnp.int32), axis=2).astype(jnp.int32)
    top_seg = jnp.full((N_SECTION,), seg_count - 1, jnp.int32)
    q_seg = jax.random.randint(query_key, (N_SECTION, TQ), 0, top_seg[:, None] + 1).astype(jnp.int32)
    token_pos = jnp.arange(TQ, dtype=jnp.int32)[None, :]
    q_seg = jnp.where(token_pos == TQ - 1, top_seg[:, None], q_seg)
    q_seg = jnp.where(token_pos % 64 == 0, 0, q_seg).astype(jnp.int32).reshape(QROWS)
    return (pack, kv_seg, q_seg)


def memory_keys(key):
    return jax.random.normal(jax.random.fold_in(key, 99), (MEM, D), jnp.float32)


def draw_keys(key, part):
    return memory_keys(key).astype(jnp.bfloat16)


def draw_queries(key, part):
    key = jax.random.fold_in(key, 5)
    drawn = jax.random.normal(key, (QROWS, D), jnp.float32)
    return drawn.astype(jnp.bfloat16)


def draw_pack(key, part):
    return packing_layout(key)[0]


def draw_kv_seg(key, part):
    return packing_layout(key)[1]


def draw_q_seg(key, part):
    return packing_layout(key)[2]


def level_of(own_key, dims, split, smallest, top_value):
    def one(position, parts):
        heights = jax.random.uniform(jax.random.fold_in(jax.random.fold_in(own_key, 6), position), (parts,), jnp.float32, smallest / len(split), top_value / len(split))
        return jnp.repeat(jnp.exp(heights), dims[position] // parts).reshape((-1,) + (1,) * (len(dims) - position - 1))

    gain = one(*split[0])
    for cut in split[1:]:
        gain = gain * one(*cut)
    return gain


def centred(key, dims, spread, limit, cuts=(), kind=jnp.bfloat16):
    result = spread * jax.random.normal(key, dims, jnp.float32)
    if cuts:
        result = result * level_of(key, dims, cuts, -0.22, 0.18)
    return jnp.clip(result, -limit, limit).astype(kind)


def setup_inputs(seed: int = 0) -> dict:
    key_list = jax.random.split(jax.random.key(seed), 9)
    queries = draw_queries(jax.random.fold_in(key_list[8], 71), 0)
    keys = draw_keys(jax.random.fold_in(key_list[8], 71), 0)
    values = centred(key_list[2], (MEM, D), 1.0, 6.0, ((0, 16), (1, 8)))
    out_weight = centred(key_list[3], (D, D), D ** -0.5, 0.09375, ((0, 8),))
    cotangent = centred(key_list[4], (QROWS, D), 1.0, 6.0, ((0, 16), (1, 8)))
    pack = draw_pack(jax.random.fold_in(key_list[8], 71), 0)
    kv_seg = draw_kv_seg(jax.random.fold_in(key_list[8], 71), 0)
    q_seg = draw_q_seg(jax.random.fold_in(key_list[8], 71), 0)
    return {"queries": queries, "keys": keys, "values": values, "out_weight": out_weight, "cotangent": cotangent, "pack": pack, "kv_seg": kv_seg, "q_seg": q_seg}


def micro_batch(query_rows, keys, values, out_weight, grad_rows, row_ids, seg_keys, seg_query):
    score_scale = HD ** -0.5
    packed_keys = jnp.take(keys, row_ids, axis=0)
    packed_values = jnp.take(values, row_ids, axis=0)
    query_heads = query_rows.reshape(TQ, H, HD).astype(jnp.float32)
    key_heads = packed_keys.reshape(KV, H, HD).astype(jnp.float32)
    value_heads = packed_values.reshape(KV, H, HD).astype(jnp.float32)
    scores = jnp.einsum('qhd,khd->hqk', query_heads, key_heads) * score_scale
    allowed = seg_query[:, None] == seg_keys[None, :]
    scores = jnp.where(allowed[None], scores, -1e30)
    top_score = jnp.max(scores, axis=-1, keepdims=True)
    raised = jnp.exp(scores - top_score)
    weights_f = raised / jnp.sum(raised, axis=-1, keepdims=True)
    weights_b = lax.optimization_barrier(weights_f.astype(jnp.bfloat16)).astype(jnp.float32)
    attn = jnp.einsum('hqk,khd->qhd', weights_b, value_heads).astype(jnp.bfloat16).reshape(TQ, D)
    mixed = jnp.dot(attn, out_weight, preferred_element_type=jnp.float32).astype(jnp.bfloat16)
    d_attn = jnp.dot(grad_rows, out_weight.T, preferred_element_type=jnp.float32).astype(jnp.bfloat16)
    weight_part = jnp.dot(attn.T, grad_rows, preferred_element_type=jnp.float32)
    d_attn_heads = d_attn.reshape(TQ, H, HD).astype(jnp.float32)
    dprobs = jnp.einsum('qhd,khd->hqk', d_attn_heads, value_heads)
    dscores = weights_f * (dprobs - jnp.sum(weights_f * dprobs, axis=-1, keepdims=True))
    dscores_b = lax.optimization_barrier(dscores.astype(jnp.bfloat16)).astype(jnp.float32)
    d_query = (jnp.einsum('hqk,khd->qhd', dscores_b, key_heads) * score_scale).astype(jnp.bfloat16).reshape(TQ, D)
    d_packed_keys = (jnp.einsum('hqk,qhd->khd', dscores_b, query_heads) * score_scale).reshape(KV, D)
    d_packed_values = jnp.einsum('hqk,qhd->khd', weights_b, d_attn_heads).reshape(KV, D)
    return mixed, d_query, weight_part, d_packed_keys, d_packed_values


def reference(queries, keys, values, out_weight, cotangent, pack, kv_seg, q_seg):
    def step(totals, section_id):
        first = (section_id * TQ).astype(jnp.int32)
        query_rows = lax.dynamic_slice_in_dim(queries, first, TQ, 0)
        grad_rows = lax.dynamic_slice_in_dim(cotangent, first, TQ, 0)
        seg_query = lax.dynamic_slice_in_dim(q_seg, first, TQ, 0)
        row_ids = pack[section_id]
        mixed, d_query, weight_part, d_pk, d_pv = micro_batch(
            query_rows, keys, values, out_weight, grad_rows, row_ids, kv_seg[section_id], seg_query)
        weight_sum, key_sum, value_sum = totals
        totals = (weight_sum + weight_part, key_sum.at[row_ids].add(d_pk), value_sum.at[row_ids].add(d_pv))
        return totals, (mixed, d_query)

    start_totals = (jnp.zeros((D, D), jnp.float32), jnp.zeros((MEM, D), jnp.float32), jnp.zeros((MEM, D), jnp.float32))
    totals, stacked = lax.scan(step, start_totals, jnp.arange(N_SECTION, dtype=jnp.int32))
    mixed = stacked[0].reshape(QROWS, D)
    d_queries = stacked[1].reshape(QROWS, D)
    return mixed, d_queries, totals[1], totals[2], totals[0]
```

```python
import functools

import jax
import jax.numpy as jnp
from jax import lax
from jax.experimental import pallas as pl
from jax.experimental.pallas import tpu as pltpu
from jax.sharding import PartitionSpec as P

HD = 256
NEG = -1e30
BF = jnp.bfloat16
F32 = jnp.float32
NT = (((1,), (1,)), ((), ()))
NN = (((1,), (0,)), ((), ()))
VMEM_BYTES = 56 * 1024 * 1024


def moved(value, step):
    pairs = []
    for y in range(4):
        for z in range(4):
            for x in range(4):
                for c in range(2):
                    a, b, d, e = step(y, z, x, c)
                    pairs.append(
                        (
                            (y * 4 + z) * 8 + x * 2 + c,
                            ((a % 4) * 4 + b % 4) * 8 + (d % 4) * 2 + e % 2,
                        )
                    )
    return lax.ppermute(value, ("section", "mp"), pairs)


def move_x(value, by):
    return moved(value, lambda y, z, x, c: (y, z, x + by, c))


def move_core(value):
    return moved(value, lambda y, z, x, c: (y, z, x, c + 1))


def move_first(value, by):
    return moved(value, lambda y, z, x, c: (y, z + by, x, c) if c == 0 else (y + by, z, x, c))


def move_second(value, by):
    return moved(value, lambda y, z, x, c: (y + by, z, x, c) if c == 0 else (y, z + by, x, c))


def dot(a, b, dims=NN):
    return lax.dot_general(a, b, dims, preferred_element_type=F32)


def forward_kernel(
    idx_ref, s0, s1, s2, s3, q_ref, ks_ref, qs_ref, packed_ref, attn_ref, attn_t_ref, top_ref, inv_ref
):
    rows = idx_ref.shape[0]
    width = q_ref.shape[1]
    part = s0.shape[0]
    for b in range(0, rows, 256):
        ids = idx_ref[b : b + 256, :]
        total = None
        for t, src in enumerate((s0, s1, s2, s3)):
            cols = lax.broadcasted_iota(jnp.int32, (256, part), 1) + part * t
            pick = jnp.where(ids == cols, 1.0, 0.0).astype(BF)
            got = dot(pick, src[...])
            total = got if total is None else total + got
        packed_ref[b : b + 256, :] = total.astype(BF)
    for h in range(width // HD):
        lo = h * HD
        k = packed_ref[:, lo : lo + HD]
        v_t = packed_ref[:, width + lo : width + lo + HD].T
        for b in range(0, q_ref.shape[0], 256):
            q = q_ref[b : b + 256, lo : lo + HD]
            s = dot(k, q, NT) * (HD**-0.5)
            s = jnp.where(ks_ref[...] == qs_ref[:, b : b + 256], s, NEG)
            top = jnp.max(s, axis=0, keepdims=True)
            e = jnp.exp(s - top)
            inv = 1.0 / jnp.sum(e, axis=0, keepdims=True)
            p = (e * inv).astype(BF)
            a_t = dot(v_t, p)
            attn_t_ref[lo : lo + HD, b : b + 256] = a_t.astype(BF)
            attn_ref[b : b + 256, lo : lo + HD] = a_t.T.astype(BF)
            top_ref[h : h + 1, b : b + 256] = top
            inv_ref[h : h + 1, b : b + 256] = inv


def forward(idx_col, sources, queries, ks_col, qs_row):
    rows, width = queries.shape
    kv = idx_col.shape[0]
    return pl.pallas_call(
        forward_kernel,
        out_shape=(
            jax.ShapeDtypeStruct((kv, 2 * width), BF),
            jax.ShapeDtypeStruct((rows, width), BF),
            jax.ShapeDtypeStruct((width, rows), BF),
            jax.ShapeDtypeStruct((width // HD, rows), F32),
            jax.ShapeDtypeStruct((width // HD, rows), F32),
        ),
        compiler_params=pltpu.CompilerParams(vmem_limit_bytes=VMEM_BYTES),
        name="gather_forward",
    )(idx_col, *sources, queries, ks_col, qs_row)


def backward_kernel(
    idx_ref, packed_ref, q_ref, da_ref, ks_ref, qs_ref, top_ref, inv_ref, dq_ref, o0, o1, o2, o3, ds_s, p_s, dp_s
):
    rows, width = q_ref.shape
    kv = packed_ref.shape[0]
    scale = HD**-0.5
    for h in range(width // HD):
        lo = h * HD
        k = packed_ref[:, lo : lo + HD]
        v = packed_ref[:, width + lo : width + lo + HD]
        k_t = k.T
        for b in range(0, rows, 256):
            q = q_ref[b : b + 256, lo : lo + HD]
            da = da_ref[b : b + 256, lo : lo + HD]
            s = dot(k, q, NT) * scale
            s = jnp.where(ks_ref[...] == qs_ref[:, b : b + 256], s, NEG)
            p = jnp.exp(s - top_ref[h : h + 1, b : b + 256]) * inv_ref[h : h + 1, b : b + 256]
            p_s[:, b : b + 256] = p.astype(BF)
            dp = dot(v, da, NT)
            mean = jnp.sum(p * dp, axis=0, keepdims=True)
            ds = (p * (dp - mean)).astype(BF)
            ds_s[:, b : b + 256] = ds
            dq_ref[b : b + 256, lo : lo + HD] = (dot(k_t, ds) * scale).T.astype(BF)
        dp_s[:, lo : lo + HD] = (dot(ds_s[...], q_ref[:, lo : lo + HD]) * scale).astype(BF)
        dp_s[:, width + lo : width + lo + HD] = dot(p_s[...], da_ref[:, lo : lo + HD]).astype(BF)
    part = o0.shape[0]
    for t, out in enumerate((o0, o1, o2, o3)):
        for b in range(0, part, 256):
            r = lax.broadcasted_iota(jnp.int32, (256, kv), 0) + (part * t + b)
            put = jnp.where(idx_ref[...] == r, 1.0, 0.0).astype(BF)
            out[b : b + 256, :] = dot(put, dp_s[...]).astype(BF)


def backward(idx_row, packed, queries, d_attn, ks_col, qs_row, top, inv, part):
    rows, width = queries.shape
    kv = packed.shape[0]
    piece = jax.ShapeDtypeStruct((part, 2 * width), BF)
    return pl.pallas_call(
        backward_kernel,
        out_shape=(jax.ShapeDtypeStruct((rows, width), BF), piece, piece, piece, piece),
        scratch_shapes=[
            pltpu.VMEM((kv, rows), BF),
            pltpu.VMEM((kv, rows), BF),
            pltpu.VMEM((kv, 2 * width), BF),
        ],
        compiler_params=pltpu.CompilerParams(vmem_limit_bytes=VMEM_BYTES),
        name="backward_scatter",
    )(idx_row, packed, queries, d_attn, ks_col, qs_row, top, inv)


def d_attn_kernel(has_acc, last, tbl, *refs):
    refs = list(refs)
    own, mate, w = refs[:3]
    acc = refs[3] if has_acc else None
    out, cot = refs[-2:]
    even = tbl[1] == 0
    width = own.shape[1]
    o, m = own[...], mate[...]
    left = jnp.where(even, o, m)
    right = jnp.where(even, m, o)
    cot[0, :, :width] = left
    cot[0, :, width:] = right
    got = dot(left, w[:, :width], NT) + dot(right, w[:, width:], NT)
    if has_acc:
        got = got + acc[...]
    out[...] = got.astype(out.dtype)


def d_attn_part(tbl, own, mate, w, acc, cot_all, last):
    rows, width = own.shape
    heads = w.shape[0]
    tm = 256
    has_acc = acc is not None
    in_specs = [
        pl.BlockSpec((tm, width), lambda i, t: (i, 0)),
        pl.BlockSpec((tm, width), lambda i, t: (i, 0)),
        pl.BlockSpec((heads, 2 * width), lambda i, t: (0, t[0])),
    ]
    operands = [own, mate, w]
    aliases = {}
    if has_acc:
        in_specs += [
            pl.BlockSpec((tm, heads), lambda i, t: (i, 0)),
            pl.BlockSpec(memory_space=pl.ANY),
        ]
        operands += [acc, cot_all]
        aliases = {5: 1}
    return pl.pallas_call(
        functools.partial(d_attn_kernel, has_acc, last),
        out_shape=(
            jax.ShapeDtypeStruct((rows, heads), BF if last else F32),
            jax.ShapeDtypeStruct((4, rows, 2 * width), BF),
        ),
        grid_spec=pltpu.PrefetchScalarGridSpec(
            num_scalar_prefetch=1,
            grid=(rows // tm,),
            in_specs=in_specs,
            out_specs=(
                pl.BlockSpec((tm, heads), lambda i, t: (i, 0)),
                pl.BlockSpec((1, tm, 2 * width), lambda i, t: (t[0], i, 0)),
            ),
        ),
        input_output_aliases=aliases,
        compiler_params=pltpu.CompilerParams(vmem_limit_bytes=VMEM_BYTES),
        name="d_attn_part",
    )(tbl, *operands)


def weight_kernel(tbl, a_ref, g_ref, out_ref):
    out_ref[...] = dot(a_ref[...], g_ref[0]).astype(out_ref.dtype)


def weight_part(tbl, attn_t, cot_all):
    heads, rows = attn_t.shape
    n = tbl.shape[0]
    width = 256
    per = cot_all.shape[2] // width
    return pl.pallas_call(
        weight_kernel,
        out_shape=jax.ShapeDtypeStruct((n * heads, width), BF),
        grid_spec=pltpu.PrefetchScalarGridSpec(
            num_scalar_prefetch=1,
            grid=(n,),
            in_specs=[
                pl.BlockSpec((heads, rows), lambda i, t: (0, 0)),
                pl.BlockSpec((1, rows, width), lambda i, t: (t[i] // per, 0, t[i] % per)),
            ],
            out_specs=pl.BlockSpec((heads, width), lambda i, t: (i, 0)),
        ),
        compiler_params=pltpu.CompilerParams(vmem_limit_bytes=VMEM_BYTES),
        name="weight_part",
    )(tbl, attn_t, cot_all)


def mixed_kernel(tbl, a_ref, b_ref, w_ref, v_ref, out_ref):
    out_ref[...] = (dot(a_ref[...], w_ref[...]) + dot(b_ref[...], v_ref[...])).astype(out_ref.dtype)


def mixed_part(tbl, attn, attn_mate, w, w_mate, kind):
    rows, heads = attn.shape
    width = 512
    tm = 256
    return pl.pallas_call(
        mixed_kernel,
        out_shape=jax.ShapeDtypeStruct((rows, width), kind),
        grid_spec=pltpu.PrefetchScalarGridSpec(
            num_scalar_prefetch=1,
            grid=(rows // tm,),
            in_specs=[
                pl.BlockSpec((tm, heads), lambda i, t: (i, 0)),
                pl.BlockSpec((tm, heads), lambda i, t: (i, 0)),
                pl.BlockSpec((heads, width), lambda i, t: (0, t[0])),
                pl.BlockSpec((heads, width), lambda i, t: (0, t[1])),
            ],
            out_specs=pl.BlockSpec((tm, width), lambda i, t: (i, 0)),
        ),
        compiler_params=pltpu.CompilerParams(vmem_limit_bytes=VMEM_BYTES),
        name="mixed_part",
    )(tbl, attn, attn_mate, w, w_mate)


def copy_kernel(tbl, a_ref, out_ref):
    out_ref[...] = a_ref[...]


def columns_for_mate(tbl, w):
    heads, cols = w.shape
    width = 512
    return pl.pallas_call(
        copy_kernel,
        out_shape=jax.ShapeDtypeStruct((heads, cols // 2), w.dtype),
        grid_spec=pltpu.PrefetchScalarGridSpec(
            num_scalar_prefetch=1,
            grid=(cols // width // 2,),
            in_specs=[pl.BlockSpec((heads, width), lambda i, t: (0, 2 * i + t[0]))],
            out_specs=pl.BlockSpec((heads, width), lambda i, t: (0, i)),
        ),
        name="columns_for_mate",
    )(tbl, w)


def f(v):
    return v.astype(F32)


def on_device(queries, keys, values, out_weight, cotangent, pack, kv_seg, q_seg):
    s = lax.axis_index("section").astype(jnp.int32)
    m = lax.axis_index("mp").astype(jnp.int32)
    y, z, x, c = s // 4, s % 4, m // 2, m % 2
    first = jnp.where(c == 0, z, y)
    second = jnp.where(c == 0, y, z)
    mem = keys.shape[0]
    width = queries.shape[1]

    r = pack[0]
    ry, rz = r // (4 * mem), (r // mem) % 4
    k1 = (jnp.where(c == 0, rz, ry) - first) % 4
    k2 = (jnp.where(c == 0, ry, rz) - second) % 4
    idx = (k2 * 4 + k1) * mem + r % mem
    idx_col, idx_row = idx[:, None], idx[None, :]
    ks_col, qs_row = kv_seg[0][:, None], q_seg[None, :]

    kv = jnp.concatenate((keys, values), axis=1)
    near = [kv] + [move_first(kv, -k) for k in (1, 2, 3)]
    from_next, from_last = move_x(cotangent, -1), move_x(cotangent, 1)
    half = cotangent.shape[0] // 2
    near = jnp.concatenate(near, axis=0)
    sources = [near] + [move_second(near, -k) for k in (1, 2, 3)]
    far_top = move_x(from_next[:half], -1)
    far_low = move_x(from_last[half:], 1)
    far = jnp.concatenate((far_top, far_low), axis=0)
    blocks = [cotangent, from_next, far, from_last]

    w_mate = move_core(columns_for_mate((1 - c)[None], out_weight))

    acc, cot_all = None, None
    for n, k in enumerate((0, 1, 3, 2)):
        tbl = jnp.stack(((x + k) % 4, c))
        acc, cot_all = d_attn_part(tbl, blocks[k], move_core(blocks[k]), out_weight, acc, cot_all, n == 3)
    d_attn = acc

    packed, attn, attn_t, top, inv = forward(idx_col, sources, queries, ks_col, qs_row)
    attn_mate = move_core(attn)

    got = []
    for k in (2, 1, 3):
        to = (x + k) % 4
        part = mixed_part(jnp.stack((2 * to + c, to)), attn, attn_mate, out_weight, w_mate, BF)
        got.append(move_x(part, k))
    own = mixed_part(jnp.stack((2 * x + c, x)), attn, attn_mate, out_weight, w_mate, F32)
    mixed = (own + f(got[0]) + f(got[1]) + f(got[2])).astype(BF)

    def sections(k2):
        a1 = (first + jnp.arange(4, dtype=jnp.int32)) % 4
        a2 = (second + k2) % 4
        return jnp.where(c == 0, a2 * 4 + a1, a1 * 4 + a2)

    w_got = [move_second(weight_part(sections(k), attn_t, cot_all), k) for k in (2, 1, 3)]
    w_got.append(weight_part(sections(0), attn_t, cot_all))

    def reduce_first(pieces, rows):
        sums = []
        for k in (0, 1, 2, 3):
            lo = k * rows
            sums.append(sum(f(v[lo : lo + rows]) for v in pieces))
        moves = [move_first(sums[k].astype(BF), k) for k in (1, 2, 3)]
        return sums[0] + f(moves[0]) + f(moves[1]) + f(moves[2])

    d_out_weight = reduce_first(w_got, width)

    d_queries, *pieces = backward(idx_row, packed, queries, d_attn, ks_col, qs_row, top, inv, 4 * mem)
    d_got = [move_second(pieces[k], k) for k in (2, 1, 3)] + [pieces[0]]
    d_kv = reduce_first(d_got, mem)
    return (mixed, d_queries, d_kv[:, :width], d_kv[:, width:], d_out_weight)


def solution(mesh):
    placed = (
        P("section", "mp"),
        P("section", "mp"),
        P("section", "mp"),
        P("mp", None),
        P("section", "mp"),
        P("section", None),
        P("section", None),
        P("section"),
    )
    return jax.shard_map(
        on_device,
        mesh=mesh,
        in_specs=placed,
        out_specs=(
            P("section", "mp"),
            P("section", "mp"),
            P("section", "mp"),
            P("section", "mp"),
            P("mp", "section"),
        ),
        check_vma=False,
    )
```

```python
import functools

import jax
import jax.numpy as jnp
from jax import lax
from jax.experimental import pallas as pl
from jax.experimental.pallas import tpu as pltpu
from jax.sharding import PartitionSpec as P

HD = 256
NEG = -1e30
BF = jnp.bfloat16
F32 = jnp.float32
NT = (((1,), (1,)), ((), ()))
NN = (((1,), (0,)), ((), ()))
VMEM_BYTES = 56 * 1024 * 1024


def moved(value, step):
    pairs = []
    for y in range(4):
        for z in range(4):
            for x in range(4):
                for c in range(2):
                    a, b, d, e = step(y, z, x, c)
                    pairs.append(
                        (
                            (y * 4 + z) * 8 + x * 2 + c,
                            ((a % 4) * 4 + b % 4) * 8 + (d % 4) * 2 + e % 2,
                        )
                    )
    return lax.ppermute(value, ("section", "mp"), pairs)


def move_first(value, by):
    return moved(value, lambda y, z, x, c: (y, z + by, x, c) if c == 0 else (y + by, z, x, c))


def move_second(value, by):
    return moved(value, lambda y, z, x, c: (y + by, z, x, c) if c == 0 else (y, z + by, x, c))


def dot(a, b, dims=NN):
    return lax.dot_general(a, b, dims, preferred_element_type=F32)


BLK = 256


def meets(bounds, t, b):
    return jnp.logical_and(bounds[t] < (b + 1) * BLK, bounds[t + 1] > b * BLK)


def forward_kernel(
    bounds, rank_ref, s0, s1, s2, s3, q_ref, ks_ref, qs_ref,
    packed_out, attn_ref, attn_t_ref, top_ref, inv_ref,
    src, acc, packed_ref, in_sem, out_sem,
):
    rows, width = q_ref.shape
    kv = packed_ref.shape[0]
    part = s0.shape[0]
    loads = [pltpu.make_async_copy(s, src.at[t], in_sem.at[t]) for t, s in enumerate((s0, s1, s2, s3))]
    for load in loads:
        load.start()
    acc[...] = jnp.zeros_like(acc)
    per = part // BLK
    for t in range(4 * per):
        if t % per == 0:
            loads[t // per].wait()
        for b in range(kv // BLK):

            @pl.when(meets(bounds, t, b))
            def _():
                at = rank_ref[:, t * BLK : (t + 1) * BLK]
                want = lax.broadcasted_iota(jnp.int32, (BLK, BLK), 0) + b * BLK
                pick = jnp.where(at == want, 1.0, 0.0).astype(BF)
                rows_in = src[t // per, (t % per) * BLK : (t % per + 1) * BLK, :]
                acc[b * BLK : (b + 1) * BLK, :] += dot(pick, rows_in)

    packed_ref[...] = acc[...].astype(BF)
    store = pltpu.make_async_copy(packed_ref, packed_out, out_sem)
    store.start()
    for h in range(width // HD):
        lo = h * HD
        k = packed_ref[:, lo : lo + HD]
        v_t = packed_ref[:, width + lo : width + lo + HD].T
        for b in range(0, rows, BLK):
            q = q_ref[b : b + BLK, lo : lo + HD]
            s = dot(k, q, NT) * (HD**-0.5)
            s = jnp.where(ks_ref[...] == qs_ref[:, b : b + BLK], s, NEG)
            top = jnp.max(s, axis=0, keepdims=True)
            e = jnp.exp(s - top)
            inv = 1.0 / jnp.sum(e, axis=0, keepdims=True)
            p = (e * inv).astype(BF)
            a_t = dot(v_t, p)
            attn_t_ref[lo : lo + HD, b : b + BLK] = a_t.astype(BF)
            attn_ref[b : b + BLK, lo : lo + HD] = a_t.T.astype(BF)
            top_ref[h : h + 1, b : b + BLK] = top
            inv_ref[h : h + 1, b : b + BLK] = inv
    store.wait()


ANY = pl.BlockSpec(memory_space=pl.ANY)
WHOLE = pl.BlockSpec(memory_space=pltpu.VMEM)
SCALARS = pl.BlockSpec(memory_space=pltpu.SMEM)


def forward(bounds, rank_row, sources, queries, ks_col, qs_row):
    rows, width = queries.shape
    kv = ks_col.shape[0]
    part = sources[0].shape[0]
    return pl.pallas_call(
        forward_kernel,
        out_shape=(
            jax.ShapeDtypeStruct((kv, 2 * width), BF),
            jax.ShapeDtypeStruct((rows, width), BF),
            jax.ShapeDtypeStruct((width, rows), BF),
            jax.ShapeDtypeStruct((width // HD, rows), F32),
            jax.ShapeDtypeStruct((width // HD, rows), F32),
        ),
        in_specs=[SCALARS, WHOLE] + [ANY] * 4 + [WHOLE] * 3,
        out_specs=(ANY,) + (WHOLE,) * 4,
        scratch_shapes=[
            pltpu.VMEM((4, part, 2 * width), BF),
            pltpu.VMEM((kv, 2 * width), F32),
            pltpu.VMEM((kv, 2 * width), BF),
            pltpu.SemaphoreType.DMA((4,)),
            pltpu.SemaphoreType.DMA,
        ],
        compiler_params=pltpu.CompilerParams(vmem_limit_bytes=VMEM_BYTES),
        name="gather_forward",
    )(bounds, rank_row, *sources, queries, ks_col, qs_row)


def backward_kernel(
    bounds, rank_ref, packed_ref, q_ref, da_ref, ks_ref, qs_ref, top_ref, inv_ref,
    dq_ref, o0, o1, o2, o3,
    ds_s, p_s, dp_s, acc, piece, sem,
):
    rows, width = q_ref.shape
    kv = packed_ref.shape[0]
    scale = HD**-0.5
    for h in range(width // HD):
        lo = h * HD
        k = packed_ref[:, lo : lo + HD]
        v = packed_ref[:, width + lo : width + lo + HD]
        k_t = k.T
        for b in range(0, rows, BLK):
            q = q_ref[b : b + BLK, lo : lo + HD]
            da = da_ref[b : b + BLK, lo : lo + HD]
            s = dot(k, q, NT) * scale
            s = jnp.where(ks_ref[...] == qs_ref[:, b : b + BLK], s, NEG)
            p = jnp.exp(s - top_ref[h : h + 1, b : b + BLK]) * inv_ref[h : h + 1, b : b + BLK]
            p_s[:, b : b + BLK] = p.astype(BF)
            dp = dot(v, da, NT)
            mean = jnp.sum(p * dp, axis=0, keepdims=True)
            ds = (p * (dp - mean)).astype(BF)
            ds_s[:, b : b + BLK] = ds
            dq_ref[b : b + BLK, lo : lo + HD] = (dot(k_t, ds) * scale).T.astype(BF)
        dp_s[:, lo : lo + HD] = (dot(ds_s[...], q_ref[:, lo : lo + HD]) * scale).astype(BF)
        dp_s[:, width + lo : width + lo + HD] = dot(p_s[...], da_ref[:, lo : lo + HD]).astype(BF)
    part = o0.shape[0]
    per = part // BLK
    outs = (o0, o1, o2, o3)
    stores = [pltpu.make_async_copy(piece.at[t], outs[t], sem.at[t]) for t in range(4)]
    for n in (2, 1, 3, 0):
        for u in range(per):
            t = n * per + u
            acc[...] = jnp.zeros_like(acc)
            for b in range(kv // BLK):

                @pl.when(meets(bounds, t, b))
                def _():
                    at = rank_ref[t * BLK : (t + 1) * BLK, :]
                    have = lax.broadcasted_iota(jnp.int32, (BLK, BLK), 1) + b * BLK
                    put = jnp.where(at == have, 1.0, 0.0).astype(BF)
                    acc[...] += dot(put, dp_s[b * BLK : (b + 1) * BLK, :])

            piece[n, u * BLK : (u + 1) * BLK, :] = acc[...].astype(BF)
        stores[n].start()
    for store in stores:
        store.wait()


def backward(bounds, rank_col, packed, queries, d_attn, ks_col, qs_row, top, inv, part):
    rows, width = queries.shape
    kv = packed.shape[0]
    piece = jax.ShapeDtypeStruct((part, 2 * width), BF)
    return pl.pallas_call(
        backward_kernel,
        out_shape=(jax.ShapeDtypeStruct((rows, width), BF), piece, piece, piece, piece),
        in_specs=[SCALARS] + [WHOLE] * 8,
        out_specs=(WHOLE,) + (ANY,) * 4,
        scratch_shapes=[
            pltpu.VMEM((kv, rows), BF),
            pltpu.VMEM((kv, rows), BF),
            pltpu.VMEM((kv, 2 * width), BF),
            pltpu.VMEM((BLK, 2 * width), F32),
            pltpu.VMEM((4, part, 2 * width), BF),
            pltpu.SemaphoreType.DMA((4,)),
        ],
        compiler_params=pltpu.CompilerParams(vmem_limit_bytes=VMEM_BYTES),
        name="backward_scatter",
    )(bounds, rank_col, packed, queries, d_attn, ks_col, qs_row, top, inv)


def d_attn_kernel(a0, a1, w_ref, out_ref, acc):
    i = pl.program_id(0)
    width = a0.shape[1]
    got = dot(a0[...], w_ref[:, :width], NT) + dot(a1[...], w_ref[:, width:], NT)

    @pl.when(i == 0)
    def _():
        acc[...] = got

    @pl.when(i > 0)
    def _():
        acc[...] += got

    @pl.when(i == pl.num_programs(0) - 1)
    def _():
        out_ref[...] = acc[...].astype(out_ref.dtype)


def d_attn_of(full_grad, w, rows):
    heads, cols = w.shape
    width = full_grad.shape[1]
    return pl.pallas_call(
        d_attn_kernel,
        out_shape=jax.ShapeDtypeStruct((rows, heads), BF),
        grid=(cols // width // 2,),
        in_specs=[
            pl.BlockSpec((rows, width), lambda i: (2 * i, 0)),
            pl.BlockSpec((rows, width), lambda i: (2 * i + 1, 0)),
            pl.BlockSpec((heads, 2 * width), lambda i: (0, i)),
        ],
        out_specs=pl.BlockSpec((rows, heads), lambda i: (0, 0)),
        scratch_shapes=[pltpu.VMEM((rows, heads), F32)],
        compiler_params=pltpu.CompilerParams(vmem_limit_bytes=VMEM_BYTES),
        name="d_attn",
    )(full_grad, full_grad, w)


def weight_kernel(n, tbl, a_ref, g_ref, *outs):
    got = dot(a_ref[...], g_ref[...]).astype(BF)
    for k in range(n):

        @pl.when(pl.program_id(0) // 4 == k)
        def _():
            outs[k][...] = got


def weight_pieces(tbl, attn_t, full_grad, offsets):
    heads, rows = attn_t.shape
    n = len(offsets)
    width = 256
    per = full_grad.shape[1] // width
    first = offsets[0]
    step = offsets[1] - first if n > 1 else 0
    sec = lambda i, t: t[(first + step * (i // 4)) * 4 + i % 4]
    return pl.pallas_call(
        functools.partial(weight_kernel, n),
        out_shape=(jax.ShapeDtypeStruct((4 * heads, width), BF),) * n,
        grid_spec=pltpu.PrefetchScalarGridSpec(
            num_scalar_prefetch=1,
            grid=(4 * n,),
            in_specs=[
                pl.BlockSpec((heads, rows), lambda i, t: (0, 0)),
                pl.BlockSpec((rows, width), lambda i, t: (sec(i, t) // per, sec(i, t) % per)),
            ],
            out_specs=tuple(
                pl.BlockSpec((heads, width), functools.partial(lambda k, i, t: (jnp.clip(i - 4 * k, 0, 3), 0), k))
                for k in range(n)
            ),
        ),
        compiler_params=pltpu.CompilerParams(vmem_limit_bytes=VMEM_BYTES),
        name="weight_pieces",
    )(tbl, attn_t, full_grad)


def mixed_kernel(a_ref, w_ref, out_ref):
    out_ref[...] = dot(a_ref[...], w_ref[...]).astype(out_ref.dtype)


def mixed_partial(attn, w):
    rows, heads = attn.shape
    width = 512
    n = w.shape[1] // width
    return pl.pallas_call(
        mixed_kernel,
        out_shape=jax.ShapeDtypeStruct((n * rows, width), BF),
        grid=(n,),
        in_specs=[
            pl.BlockSpec((rows, heads), lambda i: (0, 0)),
            pl.BlockSpec((heads, width), lambda i: (0, i)),
        ],
        out_specs=pl.BlockSpec((rows, width), lambda i: (i, 0)),
        compiler_params=pltpu.CompilerParams(vmem_limit_bytes=VMEM_BYTES),
        name="mixed_partial",
    )(attn, w)


def f(v):
    return v.astype(F32)


def on_device(queries, keys, values, out_weight, cotangent, pack, kv_seg, q_seg):
    s = lax.axis_index("section").astype(jnp.int32)
    c = lax.axis_index("mp").astype(jnp.int32) % 2
    y, z = s // 4, s % 4
    first = jnp.where(c == 0, z, y)
    second = jnp.where(c == 0, y, z)
    mem = keys.shape[0]
    rows, width = queries.shape

    kv = jnp.concatenate((keys, values), axis=1)
    near = [kv] + [move_first(kv, -k) for k in (1, 2, 3)]
    near = jnp.concatenate(near, axis=0)
    sources = [near] + [move_second(near, -k) for k in (1, 2, 3)]

    full_grad = lax.all_gather(cotangent, "mp", axis=0, tiled=True)

    r = pack[0]
    ry, rz = r // (4 * mem), (r // mem) % 4
    k1 = (jnp.where(c == 0, rz, ry) - first) % 4
    k2 = (jnp.where(c == 0, ry, rz) - second) % 4
    idx = (k2 * 4 + k1) * mem + r % mem
    rank = jnp.sum((idx[None, :] < idx[:, None]).astype(jnp.int32), axis=1)
    places = jnp.arange(16 * mem, dtype=jnp.int32)
    rank_of = jnp.max(jnp.where(idx[:, None] == places[None, :], rank[:, None], -1), axis=0)
    order = jnp.arange(r.shape[0], dtype=jnp.int32)
    seg = jnp.sum(jnp.where(rank[:, None] == order[None, :], kv_seg[0][:, None], 0), axis=0)
    starts = jnp.arange(0, 16 * mem + 1, BLK, dtype=jnp.int32)
    bounds = jnp.sum((idx[None, :] < starts[:, None]).astype(jnp.int32), axis=1)
    ks_col, qs_row = seg[:, None], q_seg[None, :]

    d = jnp.arange(16, dtype=jnp.int32)
    a1, a2 = (first + d % 4) % 4, (second + d // 4) % 4
    sections = jnp.where(c == 0, a2 * 4 + a1, a1 * 4 + a2)

    packed, attn, attn_t, top, inv = forward(bounds, rank_of[None, :], sources, queries, ks_col, qs_row)

    mixed = lax.psum_scatter(mixed_partial(attn, out_weight), "mp", scatter_dimension=0, tiled=True)

    w_pieces = weight_pieces(sections, attn_t, full_grad, (1, 2, 3))
    w_got = [move_second(w_pieces[k - 1], k) for k in (2, 1, 3)]
    w_got.append(weight_pieces(sections, attn_t, full_grad, (0,))[0])

    def reduce_first(pieces, rows):
        sums = []
        for k in (0, 1, 2, 3):
            lo = k * rows
            sums.append(sum(f(v[lo : lo + rows]) for v in pieces))
        moves = [move_first(sums[k].astype(BF), k) for k in (1, 2, 3)]
        return sums[0] + f(moves[0]) + f(moves[1]) + f(moves[2])

    d_attn = d_attn_of(full_grad, out_weight, rows)
    d_queries, *pieces = backward(
        bounds, rank_of[:, None], packed, queries, d_attn, ks_col, qs_row, top, inv, 4 * mem
    )
    d_got = [move_second(pieces[k], k) for k in (2, 1, 3)] + [pieces[0]]
    d_out_weight = reduce_first(w_got, width)
    d_kv = reduce_first(d_got, mem)
    return (mixed, d_queries, d_kv[:, :width], d_kv[:, width:], d_out_weight)


def solution(mesh):
    placed = (
        P("section", "mp"),
        P("section", "mp"),
        P("section", "mp"),
        P("mp", None),
        P("section", "mp"),
        P("section", None),
        P("section", None),
        P("section"),
    )
    return jax.shard_map(
        on_device,
        mesh=mesh,
        in_specs=placed,
        out_specs=(
            P("section", "mp"),
            P("section", "mp"),
            P("section", "mp"),
            P("section", "mp"),
            P("mp", "section"),
        ),
        check_vma=False,
    )
```

```python
import functools

import jax
import jax.numpy as jnp
from jax import lax
from jax.experimental import pallas as pl
from jax.experimental.pallas import tpu as pltpu
from jax.sharding import PartitionSpec as P

HD = 256
NEG = -1e30
BF = jnp.bfloat16
F32 = jnp.float32
NT = (((1,), (1,)), ((), ()))
NN = (((1,), (0,)), ((), ()))
VMEM_BYTES = 56 * 1024 * 1024


def moved(value, step):
    pairs = []
    for y in range(4):
        for z in range(4):
            for x in range(4):
                for c in range(2):
                    a, b, d, e = step(y, z, x, c)
                    pairs.append(
                        (
                            (y * 4 + z) * 8 + x * 2 + c,
                            ((a % 4) * 4 + b % 4) * 8 + (d % 4) * 2 + e % 2,
                        )
                    )
    return lax.ppermute(value, ("section", "mp"), pairs)


def move_core(value):
    return moved(value, lambda y, z, x, c: (y, z, x, c + 1))


def move_ahead(value):
    return moved(value, lambda y, z, x, c: (y, z, x + 1 - 2 * c, c))


def move_behind(value):
    return moved(value, lambda y, z, x, c: (y, z, x - 1 + 2 * c, c))


def move_first(value, by):
    return moved(value, lambda y, z, x, c: (y, z + by, x, c) if c == 0 else (y + by, z, x, c))


def move_second(value, by):
    return moved(value, lambda y, z, x, c: (y + by, z, x, c) if c == 0 else (y, z + by, x, c))


def dot(a, b, dims=NN):
    return lax.dot_general(a, b, dims, preferred_element_type=F32)


BLK = 256
FINE = 128
ROWS_IN = BLK + 16
ANY = pl.BlockSpec(memory_space=pl.ANY)
WHOLE = pl.BlockSpec(memory_space=pltpu.VMEM)
SCALARS = pl.BlockSpec(memory_space=pltpu.SMEM)
DMA = pltpu.SemaphoreType.DMA


def cut(ref, at, size):
    return ref.at[:, pl.ds(pl.multiple_of(at * size, size), size)]


def forward_kernel(
    bounds, secs, cols, rank_ref, s0, s1, s2, s3, q_in, ks_ref, qs_ref, g0, g1, g2, g3, g4, g5, g6, g7,
    packed_out, attn_out, top_ref, inv_ref, w0, w1, w2, w3,
    src, packed_ref, q_ref, cot, attn_ref, attn_t, weight, in_sem, q_sem, cot_sem, out_sem, w_sem,
):
    rows, width = q_ref.shape
    kv = packed_ref.shape[0]
    part = s0.shape[0]
    loads = [pltpu.make_async_copy(s, src.at[t], in_sem.at[t]) for t, s in enumerate((s0, s1, s2, s3))]
    q_load = pltpu.make_async_copy(q_in, q_ref, q_sem)
    for load in loads:
        load.start()
    q_load.start()
    cot_loads = []
    for n, g in enumerate((g0, g1, g2, g3, g4, g5, g6, g7)):
        for half in range(2):
            cot_loads.append(
                pltpu.make_async_copy(
                    g.at[:, half * BLK : (half + 1) * BLK], cot.at[2 * cols[n] + half], cot_sem.at[2 * n + half]
                )
            )
    packed_ref[...] = jnp.zeros_like(packed_ref)
    per = part // BLK
    for t in range(4 * per):
        if t % per == 0:
            loads[t // per].wait()
        start = pl.multiple_of(jnp.minimum(bounds[2 * t] // 16 * 16, kv - ROWS_IN), 16)
        at = rank_ref[:, t * BLK : (t + 1) * BLK]
        want = lax.broadcasted_iota(jnp.int32, (ROWS_IN, BLK), 0) + start
        pick = jnp.where(at == want, 1.0, 0.0).astype(BF)
        got = dot(pick, src[t // per, (t % per) * BLK : (t % per + 1) * BLK, :])
        packed_ref[pl.ds(start, ROWS_IN), :] += got.astype(BF)
    for load in cot_loads:
        load.start()
    store = pltpu.make_async_copy(packed_ref, packed_out, out_sem.at[0])
    store.start()
    q_load.wait()
    for h in range(width // HD):
        lo = h * HD
        k = packed_ref[:, lo : lo + HD]
        v_t = packed_ref[:, width + lo : width + lo + HD].T
        for b in range(0, rows, BLK):
            q = q_ref[b : b + BLK, lo : lo + HD]
            s = dot(k, q, NT) * (HD**-0.5)
            s = jnp.where(ks_ref[...] == qs_ref[:, b : b + BLK], s, NEG)
            top = jnp.max(s, axis=0, keepdims=True)
            e = jnp.exp(s - top)
            inv = 1.0 / jnp.sum(e, axis=0, keepdims=True)
            p = (e * inv).astype(BF)
            a_t = dot(v_t, p)
            attn_t[lo : lo + HD, b : b + BLK] = a_t.astype(BF)
            attn_ref[b : b + BLK, lo : lo + HD] = a_t.T.astype(BF)
            top_ref[h : h + 1, b : b + BLK] = top
            inv_ref[h : h + 1, b : b + BLK] = inv
    attn_store = pltpu.make_async_copy(attn_ref, attn_out, out_sem.at[1])
    attn_store.start()
    for load in cot_loads:
        load.wait()
    outs = (w0, w1, w2, w3)
    stores = [pltpu.make_async_copy(weight.at[k], outs[k], w_sem.at[k]) for k in range(4)]
    for k2 in (2, 1, 3, 0):
        for k1 in range(4):
            weight[k2, k1 * width : (k1 + 1) * width, :] = dot(attn_t[...], cot[secs[k2 * 4 + k1]]).astype(BF)
        stores[k2].start()
    store.wait()
    attn_store.wait()
    for w_store in stores:
        w_store.wait()


def forward(bounds, secs, cols, rank_row, sources, queries, ks_col, qs_row, grads):
    rows, width = queries.shape
    kv = ks_col.shape[0]
    part = sources[0].shape[0]
    weight = jax.ShapeDtypeStruct((4 * width, BLK), BF)
    stat = jax.ShapeDtypeStruct((width // HD, rows), F32)
    return pl.pallas_call(
        forward_kernel,
        out_shape=(
            jax.ShapeDtypeStruct((kv, 2 * width), BF),
            jax.ShapeDtypeStruct((rows, width), BF),
            stat, stat, weight, weight, weight, weight,
        ),
        in_specs=[SCALARS] * 3 + [WHOLE] + [ANY] * 5 + [WHOLE] * 2 + [ANY] * 8,
        out_specs=(ANY, ANY, WHOLE, WHOLE, ANY, ANY, ANY, ANY),
        scratch_shapes=[
            pltpu.VMEM((4, part, 2 * width), BF),
            pltpu.VMEM((kv, 2 * width), BF),
            pltpu.VMEM((rows, width), BF),
            pltpu.VMEM((16, rows, BLK), BF),
            pltpu.VMEM((rows, width), BF),
            pltpu.VMEM((width, rows), BF),
            pltpu.VMEM((4, 4 * width, BLK), BF),
            DMA((4,)),
            DMA,
            DMA((16,)),
            DMA((2,)),
            DMA((4,)),
        ],
        compiler_params=pltpu.CompilerParams(vmem_limit_bytes=VMEM_BYTES),
        name="gather_forward",
    )(bounds, secs, cols, rank_row, *sources, queries, ks_col, qs_row, *grads)


def backward_kernel(
    bounds, cols, rank_ref, packed_in, q_in, part_in, g0, g1, g2, g3, w_in, ks_ref, qs_ref, top_ref, inv_ref,
    dq_ref, o0, o1, o2, o3,
    packed_ref, q_ref, part_ref, cot, w_ref, da_ref, p_f, p_s, ds_s, dp_s, piece, in_sem, g_sem, w_sem, sem,
):
    rows, width = q_ref.shape
    kv = packed_ref.shape[0]
    scale = HD**-0.5
    n_heads = width // HD
    first = [
        pltpu.make_async_copy(packed_in, packed_ref, in_sem.at[0]),
        pltpu.make_async_copy(q_in, q_ref, in_sem.at[1]),
        pltpu.make_async_copy(part_in, part_ref, in_sem.at[2]),
    ]
    later = []
    for n, g in enumerate((g0, g1, g2, g3)):
        later.append(pltpu.make_async_copy(g, cot.at[:, n * width : (n + 1) * width], g_sem.at[n]))
        later.append(
            pltpu.make_async_copy(cut(w_in, cols[n], width), w_ref.at[:, n * width : (n + 1) * width], w_sem.at[n])
        )
    for load in first + later:
        load.start()
    first[0].wait()
    first[1].wait()
    for h in range(n_heads):
        lo = h * HD
        k = packed_ref[:, lo : lo + HD]
        for b in range(0, rows, BLK):
            s = dot(k, q_ref[b : b + BLK, lo : lo + HD], NT) * scale
            s = jnp.where(ks_ref[...] == qs_ref[:, b : b + BLK], s, NEG)
            p = jnp.exp(s - top_ref[h : h + 1, b : b + BLK]) * inv_ref[h : h + 1, b : b + BLK]
            p_f[h, :, b : b + BLK] = p
            p_s[h, :, b : b + BLK] = p.astype(BF)
    first[2].wait()
    for load in later:
        load.wait()
    for b in range(0, rows, BLK):
        rest = dot(cot[b : b + BLK, :], w_ref[...], NT)
        da_ref[b : b + BLK, :] = (part_ref[b : b + BLK, :] + rest).astype(BF)
    for h in range(n_heads):
        lo = h * HD
        k_t = packed_ref[:, lo : lo + HD].T
        v = packed_ref[:, width + lo : width + lo + HD]
        for b in range(0, rows, BLK):
            dp = dot(v, da_ref[b : b + BLK, lo : lo + HD], NT)
            p = p_f[h, :, b : b + BLK]
            mean = jnp.sum(p * dp, axis=0, keepdims=True)
            ds = (p * (dp - mean)).astype(BF)
            ds_s[h, :, b : b + BLK] = ds
            dq_ref[b : b + BLK, lo : lo + HD] = (dot(k_t, ds) * scale).T.astype(BF)
        dp_s[:, lo : lo + HD] = (dot(ds_s[h], q_ref[:, lo : lo + HD]) * scale).astype(BF)
        dp_s[:, width + lo : width + lo + HD] = dot(p_s[h], da_ref[:, lo : lo + HD]).astype(BF)
    part = o0.shape[0]
    per = part // FINE
    outs = (o0, o1, o2, o3)
    stores = [pltpu.make_async_copy(piece.at[t], outs[t], sem.at[t]) for t in range(4)]
    for n in (2, 1, 3, 0):
        for u in range(per):
            t = n * per + u
            start = pl.multiple_of(jnp.minimum(bounds[t] // FINE * FINE, kv - 2 * FINE), FINE)
            at = rank_ref[t * FINE : (t + 1) * FINE, :]
            have = lax.broadcasted_iota(jnp.int32, (FINE, 2 * FINE), 1) + start
            put = jnp.where(at == have, 1.0, 0.0).astype(BF)
            piece[n, u * FINE : (u + 1) * FINE, :] = dot(put, dp_s[pl.ds(start, 2 * FINE), :]).astype(BF)
        stores[n].start()
    for store in stores:
        store.wait()


def backward(bounds, cols, rank_col, packed, queries, partial, grads, w, ks_col, qs_row, top, inv, part):
    rows, width = queries.shape
    kv = packed.shape[0]
    n_heads = width // HD
    piece = jax.ShapeDtypeStruct((part, 2 * width), BF)
    return pl.pallas_call(
        backward_kernel,
        out_shape=(jax.ShapeDtypeStruct((rows, width), BF), piece, piece, piece, piece),
        in_specs=[SCALARS] * 2 + [WHOLE] + [ANY] * 8 + [WHOLE] * 4,
        out_specs=(WHOLE,) + (ANY,) * 4,
        scratch_shapes=[
            pltpu.VMEM((kv, 2 * width), BF),
            pltpu.VMEM((rows, width), BF),
            pltpu.VMEM((rows, width), F32),
            pltpu.VMEM((rows, 4 * width), BF),
            pltpu.VMEM((width, 4 * width), BF),
            pltpu.VMEM((rows, width), BF),
            pltpu.VMEM((n_heads, kv, rows), F32),
            pltpu.VMEM((n_heads, kv, rows), BF),
            pltpu.VMEM((n_heads, kv, rows), BF),
            pltpu.VMEM((kv, 2 * width), BF),
            pltpu.VMEM((4, part, 2 * width), BF),
            DMA((3,)),
            DMA((4,)),
            DMA((4,)),
            DMA((4,)),
        ],
        compiler_params=pltpu.CompilerParams(vmem_limit_bytes=VMEM_BYTES),
        name="backward_scatter",
    )(bounds, cols, rank_col, packed, queries, partial, *grads, w, ks_col, qs_row, top, inv)


def d_attn_kernel(cols, g0, g1, g2, g3, w_in, out_ref, cot, w_ref, g_sem, w_sem):
    width = g0.shape[1]
    loads = []
    for n, g in enumerate((g0, g1, g2, g3)):
        loads.append(pltpu.make_async_copy(g, cot.at[:, n * width : (n + 1) * width], g_sem.at[n]))
        loads.append(
            pltpu.make_async_copy(cut(w_in, cols[n], width), w_ref.at[:, n * width : (n + 1) * width], w_sem.at[n])
        )
    for load in loads:
        load.start()
    for load in loads:
        load.wait()
    for b in range(0, out_ref.shape[0], BLK):
        out_ref[b : b + BLK, :] = dot(cot[b : b + BLK, :], w_ref[...], NT)


def d_attn_partial(cols, grads, w):
    rows, width = grads[0].shape
    heads = w.shape[0]
    return pl.pallas_call(
        d_attn_kernel,
        out_shape=jax.ShapeDtypeStruct((rows, heads), F32),
        in_specs=[SCALARS] + [ANY] * 5,
        out_specs=WHOLE,
        scratch_shapes=[
            pltpu.VMEM((rows, 4 * width), BF),
            pltpu.VMEM((heads, 4 * width), BF),
            DMA((4,)),
            DMA((4,)),
        ],
        compiler_params=pltpu.CompilerParams(vmem_limit_bytes=VMEM_BYTES),
        name="d_attn_partial",
    )(cols, *grads, w)


def mixed_kernel(n, add, cols, a_in, b_in, w_in, v_in, *refs):
    extra = refs[0] if add else None
    outs = refs[add : add + n]
    a_ref, b_ref, w_ref, v_ref = refs[add + n : add + n + 4]
    bufs = refs[add + n + 4 : add + 2 * n + 4]
    sem, w_sem, v_sem, o_sem = refs[add + 2 * n + 4 :]
    width = w_ref.shape[2]
    loads = [pltpu.make_async_copy(a_in, a_ref, sem.at[0]), pltpu.make_async_copy(b_in, b_ref, sem.at[1])]
    w_loads, v_loads = [], []
    for i in range(n):
        w_loads.append(pltpu.make_async_copy(cut(w_in, cols[2 * i], width), w_ref.at[i], w_sem.at[i]))
        v_loads.append(pltpu.make_async_copy(cut(v_in, cols[2 * i + 1], width), v_ref.at[i], v_sem.at[i]))
    for load in [loads[0], w_loads[0], loads[1], v_loads[0]] + w_loads[1:] + v_loads[1:]:
        load.start()
    stores = [pltpu.make_async_copy(bufs[i], outs[i], o_sem.at[i]) for i in range(n)]
    for i in range(n):
        if i == 0:
            loads[0].wait()
            loads[1].wait()
        w_loads[i].wait()
        v_loads[i].wait()
        got = dot(a_ref[...], w_ref[i]) + dot(b_ref[...], v_ref[i])
        if add and i == 0:
            got = got + extra[...].astype(F32)
        bufs[i][...] = got.astype(bufs[i].dtype)
        stores[i].start()
    for store in stores:
        store.wait()


def mixed_pieces(cols, attn, attn_mate, w, w_mate, kinds, extra=None):
    rows, heads = attn.shape
    width = 512
    n = len(kinds)
    add = 0 if extra is None else 1
    return pl.pallas_call(
        functools.partial(mixed_kernel, n, add),
        out_shape=tuple(jax.ShapeDtypeStruct((rows, width), kind) for kind in kinds),
        in_specs=[SCALARS] + [ANY] * 4 + [WHOLE] * add,
        out_specs=(ANY,) * n,
        scratch_shapes=[
            pltpu.VMEM((rows, heads), BF),
            pltpu.VMEM((rows, heads), BF),
            pltpu.VMEM((n, heads, width), BF),
            pltpu.VMEM((n, heads, width), BF),
        ]
        + [pltpu.VMEM((rows, width), kind) for kind in kinds]
        + [DMA((2,)), DMA((n,)), DMA((n,)), DMA((n,))],
        compiler_params=pltpu.CompilerParams(vmem_limit_bytes=VMEM_BYTES),
        name="mixed_pieces",
    )(cols, attn, attn_mate, w, w_mate, *([extra] if add else []))


def mate_kernel(core, w_in, out_ref, sem):
    width = 512
    copies = [
        pltpu.make_async_copy(cut(w_in, 2 * i + 1 - core[0], width), out_ref.at[:, i * width : (i + 1) * width], sem.at[i])
        for i in range(4)
    ]
    for copy in copies:
        copy.start()
    for copy in copies:
        copy.wait()


def columns_for_mate(core, w):
    heads, cols = w.shape
    return pl.pallas_call(
        mate_kernel,
        out_shape=jax.ShapeDtypeStruct((heads, cols // 2), w.dtype),
        in_specs=[SCALARS, ANY],
        out_specs=ANY,
        scratch_shapes=[DMA((4,))],
        name="columns_for_mate",
    )(core, w)


def f(v):
    return v.astype(F32)


def after(value, *others):
    return lax.optimization_barrier((value,) + others)[0]


def on_device(queries, keys, values, out_weight, cotangent, pack, kv_seg, q_seg):
    s = lax.axis_index("section").astype(jnp.int32)
    m = lax.axis_index("mp").astype(jnp.int32)
    y, z, x, c = s // 4, s % 4, m // 2, m % 2
    first = jnp.where(c == 0, z, y)
    second = jnp.where(c == 0, y, z)
    ahead = 1 - 2 * c
    mem = keys.shape[0]
    rows, width = queries.shape

    kv = jnp.concatenate((keys, values), axis=1)
    near = [kv] + [move_first(kv, -k) for k in (1, 2, 3)]
    near = jnp.concatenate(near, axis=0)
    sources = [near] + [move_second(near, -k) for k in (1, 2, 3)]

    from_behind = move_ahead(cotangent)
    from_ahead = move_behind(after(cotangent, near))
    from_far = move_ahead(from_behind)
    own_mate = move_core(cotangent)
    w_mate = move_core(columns_for_mate(c[None], out_weight))
    behind_mate = move_core(from_behind)
    ahead_mate = move_core(from_ahead)
    far_mate = move_core(from_far)
    grads = [cotangent, own_mate, from_behind, behind_mate, from_ahead, ahead_mate, from_far, far_mate]
    xs = jnp.stack((x, x, x - ahead, x + ahead, x + ahead, x - ahead, x + 2, x + 2)) % 4
    cols = 2 * xs + jnp.stack((c, 1 - c) * 4)

    r = pack[0]
    ry, rz = r // (4 * mem), (r // mem) % 4
    k1 = (jnp.where(c == 0, rz, ry) - first) % 4
    k2 = (jnp.where(c == 0, ry, rz) - second) % 4
    idx = (k2 * 4 + k1) * mem + r % mem
    rank = jnp.sum((idx[None, :] < idx[:, None]).astype(jnp.int32), axis=1)
    places = jnp.arange(16 * mem, dtype=jnp.int32)
    rank_of = jnp.max(jnp.where(idx[:, None] == places[None, :], rank[:, None], -1), axis=0)
    order = jnp.arange(r.shape[0], dtype=jnp.int32)
    seg = jnp.sum(jnp.where(rank[:, None] == order[None, :], kv_seg[0][:, None], 0), axis=0)
    starts = jnp.arange(0, 16 * mem, FINE, dtype=jnp.int32)
    bounds = jnp.sum((idx[None, :] < starts[:, None]).astype(jnp.int32), axis=1)
    ks_col, qs_row = seg[:, None], q_seg[None, :]

    d = jnp.arange(16, dtype=jnp.int32)
    a1, a2 = (first + d % 4) % 4, (second + d // 4) % 4
    sections = jnp.where(c == 0, a2 * 4 + a1, a1 * 4 + a2)

    partial = d_attn_partial(cols[:4], grads[:4], out_weight)
    packed, attn, top, inv, w0, w1, w2, w3 = forward(
        bounds, sections, cols, rank_of[None, :], sources, queries, ks_col, qs_row, grads
    )
    attn_mate = move_core(attn)
    w_got = [move_second(w2, 2), move_second(w1, 1), move_second(w3, 3), w0]

    def pair(to):
        to = to % 4
        return jnp.stack((2 * to + c, to))

    far, behind = mixed_pieces(
        jnp.concatenate((pair(x + 2), pair(x - ahead))), attn, attn_mate, out_weight, w_mate, (BF, BF)
    )
    far_got, behind_got = move_ahead(far), move_behind(behind)

    d_queries, *pieces = backward(
        bounds, cols[4:], rank_of[:, None], packed, after(queries, far), partial, grads[4:], out_weight,
        ks_col, qs_row, top, inv, 4 * mem,
    )
    d_got = [move_second(pieces[k], k) for k in (2, 1, 3)] + [pieces[0]]

    to_ahead, own = mixed_pieces(
        jnp.concatenate((pair(x + ahead), pair(x))), attn, attn_mate, out_weight, w_mate, (BF, F32),
        extra=after(far_got, d_queries),
    )
    mixed = (own + f(move_ahead(to_ahead)) + f(behind_got)).astype(BF)

    def reduce_first(pieces, rows):
        sums = []
        for k in (0, 1, 2, 3):
            lo = k * rows
            sums.append(sum(f(v[lo : lo + rows]) for v in pieces))
        moves = [move_first(sums[k].astype(BF), k) for k in (1, 2, 3)]
        return sums[0] + f(moves[0]) + f(moves[1]) + f(moves[2])

    d_out_weight = reduce_first(w_got, width)
    d_kv = reduce_first(d_got, mem)
    return (mixed, d_queries, d_kv[:, :width], d_kv[:, width:], d_out_weight)


def solution(mesh):
    placed = (
        P("section", "mp"),
        P("section", "mp"),
        P("section", "mp"),
        P("mp", None),
        P("section", "mp"),
        P("section", None),
        P("section", None),
        P("section"),
    )
    return jax.shard_map(
        on_device,
        mesh=mesh,
        in_specs=placed,
        out_specs=(
            P("section", "mp"),
            P("section", "mp"),
            P("section", "mp"),
            P("section", "mp"),
            P("mp", "section"),
        ),
        check_vma=False,
    )
```

```python
import functools

import jax
import jax.numpy as jnp
from jax import lax
from jax.experimental import pallas as pl
from jax.experimental.pallas import tpu as pltpu
from jax.sharding import PartitionSpec as P

HD = 256
NEG = -1e30
BF = jnp.bfloat16
F32 = jnp.float32
NT = (((1,), (1,)), ((), ()))
NN = (((1,), (0,)), ((), ()))
VMEM_BYTES = 56 * 1024 * 1024


def moved(value, step):
    pairs = []
    for y in range(4):
        for z in range(4):
            for x in range(4):
                for c in range(2):
                    a, b, d, e = step(y, z, x, c)
                    pairs.append(
                        (
                            (y * 4 + z) * 8 + x * 2 + c,
                            ((a % 4) * 4 + b % 4) * 8 + (d % 4) * 2 + e % 2,
                        )
                    )
    return lax.ppermute(value, ("section", "mp"), pairs)


def move_core(value):
    return moved(value, lambda y, z, x, c: (y, z, x, c + 1))


def move_ahead(value):
    return moved(value, lambda y, z, x, c: (y, z, x + 1 - 2 * c, c))


def move_behind(value):
    return moved(value, lambda y, z, x, c: (y, z, x - 1 + 2 * c, c))


def move_first(value, by):
    return moved(value, lambda y, z, x, c: (y, z + by, x, c) if c == 0 else (y + by, z, x, c))


def move_second(value, by):
    return moved(value, lambda y, z, x, c: (y + by, z, x, c) if c == 0 else (y, z + by, x, c))


def dot(a, b, dims=NN):
    return lax.dot_general(a, b, dims, preferred_element_type=F32)


BLK = 256
FINE = 128
ROWS_IN = BLK + 16
ANY = pl.BlockSpec(memory_space=pl.ANY)
WHOLE = pl.BlockSpec(memory_space=pltpu.VMEM)
SCALARS = pl.BlockSpec(memory_space=pltpu.SMEM)
DMA = pltpu.SemaphoreType.DMA


def cut(ref, at, size):
    return ref.at[:, pl.ds(pl.multiple_of(at * size, size), size)]


def forward_kernel(
    bounds, rank_ref, s0, s1, s2, s3, q_in, ks_ref, qs_ref,
    packed_out, attn_ref, attn_t, top_ref, inv_ref,
    src, packed_ref, q_ref, in_sem, q_sem, out_sem,
):
    rows, width = q_ref.shape
    kv = packed_ref.shape[0]
    part = s0.shape[0]
    loads = [pltpu.make_async_copy(s, src.at[t], in_sem.at[t]) for t, s in enumerate((s0, s1, s2, s3))]
    q_load = pltpu.make_async_copy(q_in, q_ref, q_sem)
    for load in loads:
        load.start()
    q_load.start()
    packed_ref[...] = jnp.zeros_like(packed_ref)
    per = part // BLK
    for t in range(4 * per):
        if t % per == 0:
            loads[t // per].wait()
        start = pl.multiple_of(jnp.minimum(bounds[2 * t] // 16 * 16, kv - ROWS_IN), 16)
        at = rank_ref[:, t * BLK : (t + 1) * BLK]
        want = lax.broadcasted_iota(jnp.int32, (ROWS_IN, BLK), 0) + start
        pick = jnp.where(at == want, 1.0, 0.0).astype(BF)
        got = dot(pick, src[t // per, (t % per) * BLK : (t % per + 1) * BLK, :])
        packed_ref[pl.ds(start, ROWS_IN), :] += got.astype(BF)
    store = pltpu.make_async_copy(packed_ref, packed_out, out_sem)
    store.start()
    q_load.wait()
    for h in range(width // HD):
        lo = h * HD
        k = packed_ref[:, lo : lo + HD]
        v_t = packed_ref[:, width + lo : width + lo + HD].T
        for b in range(0, rows, BLK):
            q = q_ref[b : b + BLK, lo : lo + HD]
            s = dot(k, q, NT) * (HD**-0.5)
            s = jnp.where(ks_ref[...] == qs_ref[:, b : b + BLK], s, NEG)
            top = jnp.max(s, axis=0, keepdims=True)
            e = jnp.exp(s - top)
            inv = 1.0 / jnp.sum(e, axis=0, keepdims=True)
            p = (e * inv).astype(BF)
            a_t = dot(v_t, p)
            attn_t[lo : lo + HD, b : b + BLK] = a_t.astype(BF)
            attn_ref[b : b + BLK, lo : lo + HD] = a_t.T.astype(BF)
            top_ref[h : h + 1, b : b + BLK] = top
            inv_ref[h : h + 1, b : b + BLK] = inv
    store.wait()


def forward(bounds, rank_row, sources, queries, ks_col, qs_row):
    rows, width = queries.shape
    kv = ks_col.shape[0]
    part = sources[0].shape[0]
    stat = jax.ShapeDtypeStruct((width // HD, rows), F32)
    return pl.pallas_call(
        forward_kernel,
        out_shape=(
            jax.ShapeDtypeStruct((kv, 2 * width), BF),
            jax.ShapeDtypeStruct((rows, width), BF),
            jax.ShapeDtypeStruct((width, rows), BF),
            stat, stat,
        ),
        in_specs=[SCALARS] + [WHOLE] + [ANY] * 5 + [WHOLE] * 2,
        out_specs=(ANY, WHOLE, WHOLE, WHOLE, WHOLE),
        scratch_shapes=[
            pltpu.VMEM((4, part, 2 * width), BF),
            pltpu.VMEM((kv, 2 * width), BF),
            pltpu.VMEM((rows, width), BF),
            DMA((4,)),
            DMA,
            DMA,
        ],
        compiler_params=pltpu.CompilerParams(vmem_limit_bytes=VMEM_BYTES),
        name="gather_forward",
    )(bounds, rank_row, *sources, queries, ks_col, qs_row)


def weight_kernel(
    secs, cols, a_in, g0, g1, g2, g3, g4, g5, g6, g7, w0, w1, w2, w3, attn_t, cot, weight, a_sem, cot_sem, w_sem
):
    heads = attn_t.shape[0]
    loads = [pltpu.make_async_copy(a_in, attn_t, a_sem)]
    for n, g in enumerate((g0, g1, g2, g3, g4, g5, g6, g7)):
        for half in range(2):
            there = cot.at[2 * cols[n] + half]
            loads.append(pltpu.make_async_copy(g.at[:, half * BLK : (half + 1) * BLK], there, cot_sem.at[2 * n + half]))
    for load in loads:
        load.start()
    for load in loads:
        load.wait()
    outs = (w0, w1, w2, w3)
    stores = [pltpu.make_async_copy(weight.at[k], outs[k], w_sem.at[k]) for k in range(4)]
    for k2 in (2, 1, 3, 0):
        for k1 in range(4):
            got = dot(attn_t[...], cot[secs[k2 * 4 + k1]])
            weight[k2, k1 * heads : (k1 + 1) * heads, :] = got.astype(BF)
        stores[k2].start()
    for store in stores:
        store.wait()


def weight_pieces(secs, cols, attn_t, grads):
    heads, rows = attn_t.shape
    piece = jax.ShapeDtypeStruct((4 * heads, BLK), BF)
    return pl.pallas_call(
        weight_kernel,
        out_shape=(piece,) * 4,
        in_specs=[SCALARS] * 2 + [ANY] * 9,
        out_specs=(ANY,) * 4,
        scratch_shapes=[
            pltpu.VMEM((heads, rows), BF),
            pltpu.VMEM((16, rows, BLK), BF),
            pltpu.VMEM((4, 4 * heads, BLK), BF),
            DMA,
            DMA((16,)),
            DMA((4,)),
        ],
        compiler_params=pltpu.CompilerParams(vmem_limit_bytes=VMEM_BYTES),
        name="weight_pieces",
    )(secs, cols, attn_t, *grads)


def backward_kernel(
    bounds, cols, rank_ref, packed_in, q_in, g0, g1, g2, g3, g4, g5, g6, g7, w_in, ks_ref, qs_ref, top_ref, inv_ref,
    dq_ref, o0, o1, o2, o3,
    packed_ref, q_ref, cot, w_ref, da_ref, p_f, p_s, ds_s, dp_s, piece, in_sem, g_sem, w_sem, sem,
):
    rows, width = q_ref.shape
    kv = packed_ref.shape[0]
    scale = HD**-0.5
    n_heads = width // HD
    first = [
        pltpu.make_async_copy(packed_in, packed_ref, in_sem.at[0]),
        pltpu.make_async_copy(q_in, q_ref, in_sem.at[1]),
    ]
    later = []
    for n, g in enumerate((g0, g1, g2, g3, g4, g5, g6, g7)):
        later.append(pltpu.make_async_copy(g, cot.at[:, n * width : (n + 1) * width], g_sem.at[n]))
        later.append(
            pltpu.make_async_copy(cut(w_in, cols[n], width), w_ref.at[:, n * width : (n + 1) * width], w_sem.at[n])
        )
    for load in first + later:
        load.start()
    first[0].wait()
    first[1].wait()

    def weights(h, b):
        lo = h * HD
        s = dot(packed_ref[:, lo : lo + HD], q_ref[b : b + BLK, lo : lo + HD], NT) * scale
        s = jnp.where(ks_ref[...] == qs_ref[:, b : b + BLK], s, NEG)
        p = jnp.exp(s - top_ref[h : h + 1, b : b + BLK]) * inv_ref[h : h + 1, b : b + BLK]
        p_f[h, :, b : b + BLK] = p
        p_s[h, :, b : b + BLK] = p.astype(BF)

    def grads(h, b, k_t):
        lo = h * HD
        dp = dot(packed_ref[:, width + lo : width + lo + HD], da_ref[b : b + BLK, lo : lo + HD], NT)
        p = p_f[h, :, b : b + BLK]
        mean = jnp.sum(p * dp, axis=0, keepdims=True)
        ds = (p * (dp - mean)).astype(BF)
        ds_s[h, :, b : b + BLK] = ds
        dq_ref[b : b + BLK, lo : lo + HD] = (dot(k_t, ds) * scale).T.astype(BF)

    def value_grads(h, r):
        lo = h * HD
        got = dot(p_s[h, r : r + BLK, :], da_ref[:, lo : lo + HD])
        dp_s[r : r + BLK, width + lo : width + lo + HD] = got.astype(BF)

    def key_grads(h, r):
        lo = h * HD
        got = dot(ds_s[h, r : r + BLK, :], q_ref[:, lo : lo + HD])
        dp_s[r : r + BLK, lo : lo + HD] = (got * scale).astype(BF)

    for b in range(0, rows, BLK):
        weights(0, b)
    for load in later:
        load.wait()
    for b in range(0, rows, BLK):
        for h in range(1, n_heads):
            weights(h, b)
        da_ref[b : b + BLK, :] = dot(cot[b : b + BLK, :], w_ref[...], NT).astype(BF)
    for h in range(n_heads):
        k_t = packed_ref[:, h * HD : (h + 1) * HD].T
        for b in range(0, rows, BLK):
            grads(h, b, k_t)
            value_grads(h, b)
            if h > 0:
                key_grads(h - 1, b)
    for r in range(0, kv, BLK):
        key_grads(n_heads - 1, r)
    part = o0.shape[0]
    per = part // FINE
    outs = (o0, o1, o2, o3)
    stores = [pltpu.make_async_copy(piece.at[t], outs[t], sem.at[t]) for t in range(4)]
    for n in (2, 1, 3, 0):
        for u in range(per):
            t = n * per + u
            start = pl.multiple_of(jnp.minimum(bounds[t] // FINE * FINE, kv - 2 * FINE), FINE)
            at = rank_ref[t * FINE : (t + 1) * FINE, :]
            have = lax.broadcasted_iota(jnp.int32, (FINE, 2 * FINE), 1) + start
            put = jnp.where(at == have, 1.0, 0.0).astype(BF)
            piece[n, u * FINE : (u + 1) * FINE, :] = dot(put, dp_s[pl.ds(start, 2 * FINE), :]).astype(BF)
        stores[n].start()
    for store in stores:
        store.wait()


def backward(bounds, cols, rank_col, packed, queries, grads, w, ks_col, qs_row, top, inv, part):
    rows, width = queries.shape
    kv = packed.shape[0]
    n_heads = width // HD
    piece = jax.ShapeDtypeStruct((part, 2 * width), BF)
    return pl.pallas_call(
        backward_kernel,
        out_shape=(jax.ShapeDtypeStruct((rows, width), BF), piece, piece, piece, piece),
        in_specs=[SCALARS] * 2 + [WHOLE] + [ANY] * 11 + [WHOLE] * 4,
        out_specs=(WHOLE,) + (ANY,) * 4,
        scratch_shapes=[
            pltpu.VMEM((kv, 2 * width), BF),
            pltpu.VMEM((rows, width), BF),
            pltpu.VMEM((rows, 8 * width), BF),
            pltpu.VMEM((width, 8 * width), BF),
            pltpu.VMEM((rows, width), BF),
            pltpu.VMEM((n_heads, kv, rows), F32),
            pltpu.VMEM((n_heads, kv, rows), BF),
            pltpu.VMEM((n_heads, kv, rows), BF),
            pltpu.VMEM((kv, 2 * width), BF),
            pltpu.VMEM((4, part, 2 * width), BF),
            DMA((2,)),
            DMA((8,)),
            DMA((8,)),
            DMA((4,)),
        ],
        compiler_params=pltpu.CompilerParams(vmem_limit_bytes=VMEM_BYTES),
        name="backward_scatter",
    )(bounds, cols, rank_col, packed, queries, *grads, w, ks_col, qs_row, top, inv)


def mixed_kernel(n, add, cols, a_in, b_in, w_in, v_in, *refs):
    extra = refs[0] if add else None
    outs = refs[add : add + n]
    a_ref, b_ref, w_ref, v_ref = refs[add + n : add + n + 4]
    bufs = refs[add + n + 4 : add + 2 * n + 4]
    sem, w_sem, v_sem, o_sem = refs[add + 2 * n + 4 :]
    width = w_ref.shape[2]
    loads = [pltpu.make_async_copy(a_in, a_ref, sem.at[0]), pltpu.make_async_copy(b_in, b_ref, sem.at[1])]
    w_loads, v_loads = [], []
    for i in range(n):
        w_loads.append(pltpu.make_async_copy(cut(w_in, cols[2 * i], width), w_ref.at[i], w_sem.at[i]))
        v_loads.append(pltpu.make_async_copy(cut(v_in, cols[2 * i + 1], width), v_ref.at[i], v_sem.at[i]))
    for load in [loads[0], w_loads[0], loads[1], v_loads[0]] + w_loads[1:] + v_loads[1:]:
        load.start()
    stores = [pltpu.make_async_copy(bufs[i], outs[i], o_sem.at[i]) for i in range(n)]
    for i in range(n):
        if i == 0:
            loads[0].wait()
            loads[1].wait()
        w_loads[i].wait()
        v_loads[i].wait()
        got = dot(a_ref[...], w_ref[i]) + dot(b_ref[...], v_ref[i])
        if add and i == 0:
            got = got + extra[...].astype(F32)
        bufs[i][...] = got.astype(bufs[i].dtype)
        stores[i].start()
    for store in stores:
        store.wait()


def mixed_pieces(cols, attn, attn_mate, w, w_mate, kinds, extra=None):
    rows, heads = attn.shape
    width = 512
    n = len(kinds)
    add = 0 if extra is None else 1
    return pl.pallas_call(
        functools.partial(mixed_kernel, n, add),
        out_shape=tuple(jax.ShapeDtypeStruct((rows, width), kind) for kind in kinds),
        in_specs=[SCALARS] + [ANY] * 4 + [WHOLE] * add,
        out_specs=(ANY,) * n,
        scratch_shapes=[
            pltpu.VMEM((rows, heads), BF),
            pltpu.VMEM((rows, heads), BF),
            pltpu.VMEM((n, heads, width), BF),
            pltpu.VMEM((n, heads, width), BF),
        ]
        + [pltpu.VMEM((rows, width), kind) for kind in kinds]
        + [DMA((2,)), DMA((n,)), DMA((n,)), DMA((n,))],
        compiler_params=pltpu.CompilerParams(vmem_limit_bytes=VMEM_BYTES),
        name="mixed_pieces",
    )(cols, attn, attn_mate, w, w_mate, *([extra] if add else []))


def mate_kernel(core, w_in, out_ref, sem):
    width = 512
    copies = [
        pltpu.make_async_copy(cut(w_in, 2 * i + 1 - core[0], width), out_ref.at[:, i * width : (i + 1) * width], sem.at[i])
        for i in range(4)
    ]
    for copy in copies:
        copy.start()
    for copy in copies:
        copy.wait()


def columns_for_mate(core, w):
    heads, cols = w.shape
    return pl.pallas_call(
        mate_kernel,
        out_shape=jax.ShapeDtypeStruct((heads, cols // 2), w.dtype),
        in_specs=[SCALARS, ANY],
        out_specs=WHOLE,
        scratch_shapes=[DMA((4,))],
        compiler_params=pltpu.CompilerParams(vmem_limit_bytes=VMEM_BYTES),
        name="columns_for_mate",
    )(core, w)


def f(v):
    return v.astype(F32)


def after(value, *others):
    return lax.optimization_barrier((value,) + others)[0]


def on_device(queries, keys, values, out_weight, cotangent, pack, kv_seg, q_seg):
    s = lax.axis_index("section").astype(jnp.int32)
    m = lax.axis_index("mp").astype(jnp.int32)
    y, z, x, c = s // 4, s % 4, m // 2, m % 2
    first = jnp.where(c == 0, z, y)
    second = jnp.where(c == 0, y, z)
    ahead = 1 - 2 * c
    mem = keys.shape[0]
    rows, width = queries.shape

    kv = jnp.concatenate((keys, values), axis=1)
    around = [move_first(kv, -k) for k in (1, 2, 3)]
    from_behind, from_ahead = move_ahead(cotangent), move_behind(cotangent)

    xs = jnp.stack((x, x, x - ahead, x + ahead, x + ahead, x - ahead, x + 2, x + 2)) % 4
    cols = 2 * xs + jnp.stack((c, 1 - c) * 4)

    r = pack[0]
    ry, rz = r // (4 * mem), (r // mem) % 4
    k1 = (jnp.where(c == 0, rz, ry) - first) % 4
    k2 = (jnp.where(c == 0, ry, rz) - second) % 4
    idx = (k2 * 4 + k1) * mem + r % mem
    rank = jnp.sum((idx[None, :] < idx[:, None]).astype(jnp.int32), axis=1)
    places = jnp.arange(16 * mem, dtype=jnp.int32)
    rank_of = jnp.max(jnp.where(idx[:, None] == places[None, :], rank[:, None], -1), axis=0)
    order = jnp.arange(r.shape[0], dtype=jnp.int32)
    seg = jnp.sum(jnp.where(rank[:, None] == order[None, :], kv_seg[0][:, None], 0), axis=0)
    starts = jnp.arange(0, 16 * mem, FINE, dtype=jnp.int32)
    bounds = jnp.sum((idx[None, :] < starts[:, None]).astype(jnp.int32), axis=1)
    ks_col, qs_row = seg[:, None], q_seg[None, :]

    d = jnp.arange(16, dtype=jnp.int32)
    a1, a2 = (first + d % 4) % 4, (second + d // 4) % 4
    sections = jnp.where(c == 0, a2 * 4 + a1, a1 * 4 + a2)

    def pair(to):
        to = to % 4
        return jnp.stack((2 * to + c, to))

    small = (
        bounds, ks_col, rank_of[None, :], rank_of[:, None], sections, cols, pair(x + 2),
        jnp.concatenate((pair(x + ahead), pair(x - ahead), pair(x))),
    )
    w_send = columns_for_mate(c[None], out_weight)
    *around, w_send, small = lax.optimization_barrier((*around, w_send, small))
    bounds, ks_col, rank_row, rank_col, sections, cols, far_cols, near_cols = small
    near = jnp.concatenate([kv] + around, axis=0)
    sources = [near] + [move_second(near, -k) for k in (1, 2, 3)]

    from_behind, from_ahead, near = lax.optimization_barrier((from_behind, from_ahead, near))
    from_far = move_ahead(from_behind)
    own_mate = move_core(after(cotangent, from_behind))
    behind_mate = move_core(from_behind)
    ahead_mate = move_core(from_ahead)

    packed, attn, attn_t, top, inv = forward(bounds, rank_row, sources, queries, ks_col, qs_row)
    far_mate = move_core(after(from_far, attn))
    w_mate = move_core(after(w_send, attn))
    grads = (cotangent, own_mate, from_behind, behind_mate, from_ahead, ahead_mate, from_far, far_mate)
    w0, w1, w2, w3 = weight_pieces(sections, cols, attn_t, grads)
    attn_mate = move_core(after(attn, w0))
    w_got = {2: move_second(w2, 2), 1: move_second(w1, 1), 3: move_second(w3, 3)}

    (far,) = mixed_pieces(far_cols, attn, attn_mate, out_weight, w_mate, (BF,))
    far_got = move_ahead(far)

    d_queries, *pieces = backward(
        bounds, cols, rank_col, packed, queries, grads, out_weight,
        ks_col, qs_row, top, inv, 4 * mem,
    )
    far_got, *pieces = lax.optimization_barrier((far_got, *pieces))
    d_got = [move_second(pieces[k], k) for k in (2, 1, 3)] + [pieces[0]]

    to_ahead, to_behind, own = mixed_pieces(
        near_cols, attn, attn_mate, out_weight, w_mate, (BF, BF, F32), extra=far_got
    )
    mixed = (own + f(move_ahead(to_ahead)) + f(move_behind(to_behind))).astype(BF)

    def reduce_first(pieces, rows):
        sums = []
        for k in (0, 1, 2, 3):
            lo = k * rows
            sums.append(sum(f(v[lo : lo + rows]) for v in pieces))
        moves = [move_first(sums[k].astype(BF), k) for k in (1, 2, 3)]
        return sums[0] + f(moves[0]) + f(moves[1]) + f(moves[2])

    *w_list, own = lax.optimization_barrier((*w_got.values(), own))
    d_out_weight = reduce_first([*w_list, w0], width)
    d_kv = reduce_first(d_got, mem)
    return (mixed, d_queries, d_kv[:, :width], d_kv[:, width:], d_out_weight)


def solution(mesh):
    placed = (
        P("section", "mp"),
        P("section", "mp"),
        P("section", "mp"),
        P("mp", None),
        P("section", "mp"),
        P("section", None),
        P("section", None),
        P("section"),
    )
    return jax.shard_map(
        on_device,
        mesh=mesh,
        in_specs=placed,
        out_specs=(
            P("section", "mp"),
            P("section", "mp"),
            P("section", "mp"),
            P("section", "mp"),
            P("mp", "section"),
        ),
        check_vma=False,
    )
```

```python
import functools

import jax
import jax.numpy as jnp
from jax import lax
from jax.experimental import pallas as pl
from jax.experimental.pallas import tpu as pltpu
from jax.sharding import PartitionSpec as P

HD = 256
NEG = -1e30
BF = jnp.bfloat16
F32 = jnp.float32
NT = (((1,), (1,)), ((), ()))
NN = (((1,), (0,)), ((), ()))
TN = (((0,), (0,)), ((), ()))
VMEM_BYTES = 56 * 1024 * 1024


def moved(value, step):
    pairs = []
    for y in range(4):
        for z in range(4):
            for x in range(4):
                for c in range(2):
                    a, b, d, e = step(y, z, x, c)
                    pairs.append(
                        (
                            (y * 4 + z) * 8 + x * 2 + c,
                            ((a % 4) * 4 + b % 4) * 8 + (d % 4) * 2 + e % 2,
                        )
                    )
    return lax.ppermute(value, ("section", "mp"), pairs)


def move_core(value):
    return moved(value, lambda y, z, x, c: (y, z, x, c + 1))


def move_ahead(value):
    return moved(value, lambda y, z, x, c: (y, z, x + 1 - 2 * c, c))


def move_behind(value):
    return moved(value, lambda y, z, x, c: (y, z, x - 1 + 2 * c, c))


def move_first(value, by):
    return moved(value, lambda y, z, x, c: (y, z + by, x, c) if c == 0 else (y + by, z, x, c))


def move_second(value, by):
    return moved(value, lambda y, z, x, c: (y + by, z, x, c) if c == 0 else (y, z + by, x, c))


def lines(along_y):
    groups = []
    for x in range(4):
        for c in range(2):
            for o in range(4):
                at = [i * 4 + o if along_y[c] else o * 4 + i for i in range(4)]
                groups.append([p * 8 + x * 2 + c for p in at])
    return groups


FIRST = lines((False, True))
SECOND = lines((True, False))


def exchange(value, groups):
    return lax.all_to_all(value, ("section", "mp"), 0, 0, axis_index_groups=groups)


def dot(a, b, dims=NN):
    return lax.dot_general(a, b, dims, preferred_element_type=F32)


BLK = 256
FINE = 128
ROWS_IN = BLK + 16
ANY = pl.BlockSpec(memory_space=pl.ANY)
WHOLE = pl.BlockSpec(memory_space=pltpu.VMEM)
SCALARS = pl.BlockSpec(memory_space=pltpu.SMEM)
DMA = pltpu.SemaphoreType.DMA


def cut(ref, at, size):
    return ref.at[:, pl.ds(pl.multiple_of(at * size, size), size)]


def forward_kernel(
    bounds, rank_ref, src_in, q_in, ks_ref, qs_ref,
    packed_out, attn_ref, attn_t, top_ref, inv_ref,
    src, packed_ref, q_ref, in_sem, q_sem, out_sem,
):
    rows, width = q_ref.shape
    kv = packed_ref.shape[0]
    part = src_in.shape[1]
    loads = [pltpu.make_async_copy(src_in.at[t], src.at[t], in_sem.at[t]) for t in range(4)]
    q_load = pltpu.make_async_copy(q_in, q_ref, q_sem)
    for load in loads:
        load.start()
    q_load.start()
    packed_ref[...] = jnp.zeros_like(packed_ref)
    per = part // BLK
    for t in range(4 * per):
        if t % per == 0:
            loads[t // per].wait()
        start = pl.multiple_of(jnp.minimum(bounds[2 * t] // 16 * 16, kv - ROWS_IN), 16)
        at = rank_ref[:, t * BLK : (t + 1) * BLK]
        want = lax.broadcasted_iota(jnp.int32, (ROWS_IN, BLK), 0) + start
        pick = jnp.where(at == want, 1.0, 0.0).astype(BF)
        got = dot(pick, src[t // per, (t % per) * BLK : (t % per + 1) * BLK, :])
        packed_ref[pl.ds(start, ROWS_IN), :] += got.astype(BF)
    store = pltpu.make_async_copy(packed_ref, packed_out, out_sem)
    store.start()
    q_load.wait()
    for h in range(width // HD):
        lo = h * HD
        k = packed_ref[:, lo : lo + HD]
        v_t = packed_ref[:, width + lo : width + lo + HD].T
        for b in range(0, rows, BLK):
            q = q_ref[b : b + BLK, lo : lo + HD]
            s = dot(k, q, NT) * (HD**-0.5)
            s = jnp.where(ks_ref[...] == qs_ref[:, b : b + BLK], s, NEG)
            top = jnp.max(s, axis=0, keepdims=True)
            e = jnp.exp(s - top)
            inv = 1.0 / jnp.sum(e, axis=0, keepdims=True)
            p = (e * inv).astype(BF)
            a_t = dot(v_t, p)
            attn_t[lo : lo + HD, b : b + BLK] = a_t.astype(BF)
            attn_ref[b : b + BLK, lo : lo + HD] = a_t.T.astype(BF)
            top_ref[h : h + 1, b : b + BLK] = top
            inv_ref[h : h + 1, b : b + BLK] = inv
    store.wait()


def forward(bounds, rank_row, gathered_kv, queries, ks_col, qs_row):
    rows, width = queries.shape
    kv = ks_col.shape[0]
    part = gathered_kv.shape[1]
    stat = jax.ShapeDtypeStruct((width // HD, rows), F32)
    return pl.pallas_call(
        forward_kernel,
        out_shape=(
            jax.ShapeDtypeStruct((kv, 2 * width), BF),
            jax.ShapeDtypeStruct((rows, width), BF),
            jax.ShapeDtypeStruct((width, rows), BF),
            stat, stat,
        ),
        in_specs=[SCALARS] + [WHOLE] + [ANY] * 2 + [WHOLE] * 2,
        out_specs=(ANY, WHOLE, WHOLE, WHOLE, WHOLE),
        scratch_shapes=[
            pltpu.VMEM((4, part, 2 * width), BF),
            pltpu.VMEM((kv, 2 * width), BF),
            pltpu.VMEM((rows, width), BF),
            DMA((4,)),
            DMA,
            DMA,
        ],
        compiler_params=pltpu.CompilerParams(vmem_limit_bytes=VMEM_BYTES),
        name="gather_forward",
    )(bounds, rank_row, gathered_kv, queries, ks_col, qs_row)


def weight_kernel(
    secs, cols, a_in, g0, g1, g2, g3, g4, g5, g6, g7, out, attn_t, cot, weight, a_sem, cot_sem, w_sem
):
    heads = attn_t.shape[0]
    loads = [pltpu.make_async_copy(a_in, attn_t, a_sem)]
    for n, g in enumerate((g0, g1, g2, g3, g4, g5, g6, g7)):
        for half in range(2):
            there = cot.at[2 * cols[n] + half]
            loads.append(pltpu.make_async_copy(g.at[:, half * BLK : (half + 1) * BLK], there, cot_sem.at[2 * n + half]))
    for load in loads:
        load.start()
    for load in loads:
        load.wait()
    stores = [pltpu.make_async_copy(weight.at[k], out.at[k], w_sem.at[k]) for k in range(4)]
    for k2 in range(4):
        for k1 in range(4):
            got = dot(attn_t[...], cot[secs[k2 * 4 + k1]])
            weight[k2, k1 * heads : (k1 + 1) * heads, :] = got.astype(BF)
        stores[k2].start()
    for store in stores:
        store.wait()


def weight_pieces(secs, cols, attn_t, grads):
    heads, rows = attn_t.shape
    return pl.pallas_call(
        weight_kernel,
        out_shape=jax.ShapeDtypeStruct((4, 4 * heads, BLK), BF),
        in_specs=[SCALARS] * 2 + [ANY] * 9,
        out_specs=ANY,
        scratch_shapes=[
            pltpu.VMEM((heads, rows), BF),
            pltpu.VMEM((16, rows, BLK), BF),
            pltpu.VMEM((4, 4 * heads, BLK), BF),
            DMA,
            DMA((16,)),
            DMA((4,)),
        ],
        compiler_params=pltpu.CompilerParams(vmem_limit_bytes=VMEM_BYTES),
        name="weight_pieces",
    )(secs, cols, attn_t, *grads)


def backward_kernel(
    bounds, cols, rank_ref, packed_in, q_in, part_in, g0, g1, g2, g3, w_in, ks_ref, qs_ref, top_ref, inv_ref,
    dq_ref, out,
    packed_ref, q_ref, part_ref, cot, w_ref, da_ref, p_f, p_s, ds_s, dp_s, piece, in_sem, g_sem, w_sem, sem,
):
    rows, width = q_ref.shape
    kv = packed_ref.shape[0]
    scale = HD**-0.5
    n_heads = width // HD
    first = [
        pltpu.make_async_copy(packed_in, packed_ref, in_sem.at[0]),
        pltpu.make_async_copy(q_in, q_ref, in_sem.at[1]),
        pltpu.make_async_copy(part_in, part_ref, in_sem.at[2]),
    ]
    later = []
    for n, g in enumerate((g0, g1, g2, g3)):
        later.append(pltpu.make_async_copy(g, cot.at[:, n * width : (n + 1) * width], g_sem.at[n]))
        later.append(
            pltpu.make_async_copy(cut(w_in, cols[n], width), w_ref.at[:, n * width : (n + 1) * width], w_sem.at[n])
        )
    for load in first + later:
        load.start()
    first[0].wait()
    first[1].wait()

    def weights(h, b):
        lo = h * HD
        s = dot(packed_ref[:, lo : lo + HD], q_ref[b : b + BLK, lo : lo + HD], NT) * scale
        s = jnp.where(ks_ref[...] == qs_ref[:, b : b + BLK], s, NEG)
        p = jnp.exp(s - top_ref[h : h + 1, b : b + BLK]) * inv_ref[h : h + 1, b : b + BLK]
        p_f[h, :, b : b + BLK] = p
        p_s[h, :, b : b + BLK] = p.astype(BF)

    def grads(h, b, k_t):
        lo = h * HD
        dp = dot(packed_ref[:, width + lo : width + lo + HD], da_ref[b : b + BLK, lo : lo + HD], NT)
        p = p_f[h, :, b : b + BLK]
        mean = jnp.sum(p * dp, axis=0, keepdims=True)
        ds = (p * (dp - mean)).astype(BF)
        ds_s[h, :, b : b + BLK] = ds
        dq_ref[b : b + BLK, lo : lo + HD] = (dot(k_t, ds) * scale).T.astype(BF)

    def value_grads(h, r):
        lo = h * HD
        got = dot(p_s[h, r : r + BLK, :], da_ref[:, lo : lo + HD])
        dp_s[r : r + BLK, width + lo : width + lo + HD] = got.astype(BF)

    def key_grads(h, r):
        lo = h * HD
        got = dot(ds_s[h, r : r + BLK, :], q_ref[:, lo : lo + HD])
        dp_s[r : r + BLK, lo : lo + HD] = (got * scale).astype(BF)

    for b in range(0, rows, BLK):
        weights(0, b)
    first[2].wait()
    for load in later:
        load.wait()
    for b in range(0, rows, BLK):
        for h in range(1, n_heads):
            weights(h, b)
        rest = dot(cot[b : b + BLK, :], w_ref[...], NT)
        da_ref[b : b + BLK, :] = (part_ref[b : b + BLK, :] + rest).astype(BF)
    for h in range(n_heads):
        k_t = packed_ref[:, h * HD : (h + 1) * HD].T
        for b in range(0, rows, BLK):
            grads(h, b, k_t)
            value_grads(h, b)
            if h > 0:
                key_grads(h - 1, b)
    for r in range(0, kv, BLK):
        key_grads(n_heads - 1, r)
    part = out.shape[1]
    per = part // FINE
    stores = [pltpu.make_async_copy(piece.at[t], out.at[t], sem.at[t]) for t in range(4)]
    for n in range(4):
        for u in range(per):
            t = n * per + u
            start = pl.multiple_of(jnp.minimum(bounds[t] // FINE * FINE, kv - 2 * FINE), FINE)
            at = rank_ref[:, t * FINE : (t + 1) * FINE]
            have = lax.broadcasted_iota(jnp.int32, (2 * FINE, FINE), 0) + start
            put = jnp.where(at == have, 1.0, 0.0).astype(BF)
            piece[n, u * FINE : (u + 1) * FINE, :] = dot(put, dp_s[pl.ds(start, 2 * FINE), :], TN).astype(BF)
        stores[n].start()
    for store in stores:
        store.wait()


def backward(bounds, cols, rank_row, packed, queries, partial, grads, w, ks_col, qs_row, top, inv, part):
    rows, width = queries.shape
    kv = packed.shape[0]
    n_heads = width // HD
    return pl.pallas_call(
        backward_kernel,
        out_shape=(jax.ShapeDtypeStruct((rows, width), BF), jax.ShapeDtypeStruct((4, part, 2 * width), BF)),
        in_specs=[SCALARS] * 2 + [WHOLE] + [ANY] * 8 + [WHOLE] * 4,
        out_specs=(WHOLE, ANY),
        scratch_shapes=[
            pltpu.VMEM((kv, 2 * width), BF),
            pltpu.VMEM((rows, width), BF),
            pltpu.VMEM((rows, width), F32),
            pltpu.VMEM((rows, 4 * width), BF),
            pltpu.VMEM((width, 4 * width), BF),
            pltpu.VMEM((rows, width), BF),
            pltpu.VMEM((n_heads, kv, rows), F32),
            pltpu.VMEM((n_heads, kv, rows), BF),
            pltpu.VMEM((n_heads, kv, rows), BF),
            pltpu.VMEM((kv, 2 * width), BF),
            pltpu.VMEM((4, part, 2 * width), BF),
            DMA((3,)),
            DMA((4,)),
            DMA((4,)),
            DMA((4,)),
        ],
        compiler_params=pltpu.CompilerParams(vmem_limit_bytes=VMEM_BYTES),
        name="backward_scatter",
    )(bounds, cols, rank_row, packed, queries, partial, *grads, w, ks_col, qs_row, top, inv)


def d_attn_kernel(n_blocks, cols, *refs):
    grads, w_in, out_ref = refs[:n_blocks], refs[n_blocks], refs[n_blocks + 1]
    cot, w_ref, g_sem, w_sem = refs[n_blocks + 2 :]
    width = grads[0].shape[1]
    loads = []
    for n, g in enumerate(grads):
        loads.append(pltpu.make_async_copy(g, cot.at[:, n * width : (n + 1) * width], g_sem.at[n]))
        loads.append(
            pltpu.make_async_copy(cut(w_in, cols[n], width), w_ref.at[:, n * width : (n + 1) * width], w_sem.at[n])
        )
    for load in loads:
        load.start()
    for load in loads:
        load.wait()
    for b in range(0, out_ref.shape[0], BLK):
        out_ref[b : b + BLK, :] = dot(cot[b : b + BLK, :], w_ref[...], NT)


def d_attn_partial(cols, grads, w):
    rows, width = grads[0].shape
    heads = w.shape[0]
    n = len(grads)
    return pl.pallas_call(
        functools.partial(d_attn_kernel, n),
        out_shape=jax.ShapeDtypeStruct((rows, heads), F32),
        in_specs=[SCALARS] + [ANY] * (n + 1),
        out_specs=WHOLE,
        scratch_shapes=[
            pltpu.VMEM((rows, n * width), BF),
            pltpu.VMEM((heads, n * width), BF),
            DMA((n,)),
            DMA((n,)),
        ],
        compiler_params=pltpu.CompilerParams(vmem_limit_bytes=VMEM_BYTES),
        name="d_attn_partial",
    )(cols, *grads, w)


def mixed_kernel(n, add, cols, a_in, b_in, w_in, v_in, *refs):
    extra = refs[:add]
    outs = refs[add : add + n]
    a_ref, b_ref, w_ref, v_ref = refs[add + n : add + n + 4]
    bufs = refs[add + n + 4 : add + 2 * n + 4]
    sem, w_sem, v_sem, o_sem = refs[add + 2 * n + 4 :]
    width = w_ref.shape[2]
    loads = [pltpu.make_async_copy(a_in, a_ref, sem.at[0]), pltpu.make_async_copy(b_in, b_ref, sem.at[1])]
    w_loads, v_loads = [], []
    for i in range(n):
        w_loads.append(pltpu.make_async_copy(cut(w_in, cols[2 * i], width), w_ref.at[i], w_sem.at[i]))
        v_loads.append(pltpu.make_async_copy(cut(v_in, cols[2 * i + 1], width), v_ref.at[i], v_sem.at[i]))
    for load in [loads[0], w_loads[0], loads[1], v_loads[0]] + w_loads[1:] + v_loads[1:]:
        load.start()
    stores = [pltpu.make_async_copy(bufs[i], outs[i], o_sem.at[i]) for i in range(n)]
    for i in range(n):
        if i == 0:
            loads[0].wait()
            loads[1].wait()
        w_loads[i].wait()
        v_loads[i].wait()
        got = dot(a_ref[...], w_ref[i]) + dot(b_ref[...], v_ref[i])
        if i < add:
            got = got + extra[i][...].astype(F32)
        bufs[i][...] = got.astype(bufs[i].dtype)
        stores[i].start()
    for store in stores:
        store.wait()


def mixed_pieces(cols, attn, attn_mate, w, w_mate, kinds, extra=()):
    rows, heads = attn.shape
    width = 512
    n = len(kinds)
    add = len(extra)
    return pl.pallas_call(
        functools.partial(mixed_kernel, n, add),
        out_shape=tuple(jax.ShapeDtypeStruct((rows, width), kind) for kind in kinds),
        in_specs=[SCALARS] + [ANY] * 4 + [WHOLE] * add,
        out_specs=(ANY,) * n,
        scratch_shapes=[
            pltpu.VMEM((rows, heads), BF),
            pltpu.VMEM((rows, heads), BF),
            pltpu.VMEM((n, heads, width), BF),
            pltpu.VMEM((n, heads, width), BF),
        ]
        + [pltpu.VMEM((rows, width), kind) for kind in kinds]
        + [DMA((2,)), DMA((n,)), DMA((n,)), DMA((n,))],
        compiler_params=pltpu.CompilerParams(vmem_limit_bytes=VMEM_BYTES),
        name="mixed_pieces",
    )(cols, attn, attn_mate, w, w_mate, *extra)


def mate_kernel(core, w_in, out_ref, sem):
    width = 512
    copies = [
        pltpu.make_async_copy(cut(w_in, 2 * i + 1 - core[0], width), out_ref.at[:, i * width : (i + 1) * width], sem.at[i])
        for i in range(4)
    ]
    for copy in copies:
        copy.start()
    for copy in copies:
        copy.wait()


def columns_for_mate(core, w):
    heads, cols = w.shape
    return pl.pallas_call(
        mate_kernel,
        out_shape=jax.ShapeDtypeStruct((heads, cols // 2), w.dtype),
        in_specs=[SCALARS, ANY],
        out_specs=WHOLE,
        scratch_shapes=[DMA((4,))],
        compiler_params=pltpu.CompilerParams(vmem_limit_bytes=VMEM_BYTES),
        name="columns_for_mate",
    )(core, w)


def f(v):
    return v.astype(F32)


def after(value, *others):
    return lax.optimization_barrier((value,) + others)[0]


def on_device(queries, keys, values, out_weight, cotangent, pack, kv_seg, q_seg):
    p = lax.axis_index("section").astype(jnp.int32)
    m = lax.axis_index("mp").astype(jnp.int32)
    x, c = m // 2, m % 2
    ahead = 1 - 2 * c
    mem = keys.shape[0]
    width = queries.shape[1]
    first = jnp.where(c == 0, p % 4, p // 4)
    second = jnp.where(c == 0, p // 4, p % 4)

    kv = jnp.concatenate((keys, values), axis=1)
    around = [move_first(kv, -k) for k in (1, 2, 3)]
    from_behind = move_ahead(cotangent)

    xs = jnp.stack((x, x, x - ahead, x + ahead, x + ahead, x - ahead, x + 2, x + 2)) % 4
    cols = 2 * xs + jnp.stack((c, 1 - c) * 4)
    d = jnp.arange(16, dtype=jnp.int32)
    to1 = (first + d) % 4
    sections = jnp.where(c == 0, d // 4 * 4 + to1, to1 * 4 + d // 4)

    def pair(to):
        to = to % 4
        return jnp.stack((2 * to + c, to))

    small = (
        sections, cols, cols[4:], pair(x + 2), jnp.concatenate((pair(x + ahead), pair(x - ahead), pair(x))),
    )
    w_send = columns_for_mate(c[None], out_weight)
    *around, from_behind, w_send, small = lax.optimization_barrier((*around, from_behind, w_send, small))
    sections, cols, last_cols, far_cols, near_cols = small

    near = jnp.concatenate([kv] + around, axis=0)
    gathered_kv = exchange(jnp.broadcast_to(near[None], (4,) + near.shape), SECOND)

    r, near = lax.optimization_barrier((pack[0], near))
    block = r // mem
    a1 = jnp.where(c == 0, block % 4, block // 4)
    a2 = jnp.where(c == 0, block // 4, block % 4)
    idx = (a2 * 4 + (a1 - first) % 4) * mem + r % mem
    rank = jnp.sum((idx[None, :] < idx[:, None]).astype(jnp.int32), axis=1)
    places = jnp.arange(16 * mem, dtype=jnp.int32)
    rank_row = jnp.max(jnp.where(idx[:, None] == places[None, :], rank[:, None], -1), axis=0)[None, :]
    order = jnp.arange(r.shape[0], dtype=jnp.int32)
    seg = jnp.sum(jnp.where(rank[:, None] == order[None, :], kv_seg[0][:, None], 0), axis=0)
    starts = jnp.arange(0, 16 * mem, FINE, dtype=jnp.int32)
    bounds = jnp.sum((idx[None, :] < starts[:, None]).astype(jnp.int32), axis=1)
    ks_col, qs_row = seg[:, None], q_seg[None, :]

    from_far, from_ahead = move_ahead(from_behind), move_behind(after(cotangent, near))
    own_mate = move_core(after(cotangent, near))
    behind_mate = move_core(from_behind)
    grads = (cotangent, own_mate, from_behind, behind_mate)
    partial = d_attn_partial(cols[:4], grads, out_weight)
    bounds, ks_col, rank_row, partial, from_ahead, from_far = lax.optimization_barrier(
        (bounds, ks_col, rank_row, partial, from_ahead, from_far)
    )
    bounds, ahead_mate, far_mate = lax.optimization_barrier((bounds, move_core(from_ahead), move_core(from_far)))

    packed, attn, attn_t, top, inv = forward(bounds, rank_row, gathered_kv, queries, ks_col, qs_row)
    last = (from_ahead, ahead_mate, from_far, far_mate)
    w_mate = move_core(after(w_send, attn))
    pieces = weight_pieces(sections, cols, attn_t, grads + last)
    pieces, attn_mate, w_mate = lax.optimization_barrier((pieces, move_core(attn), w_mate))
    w_got = exchange(pieces, SECOND)

    (far,) = mixed_pieces(far_cols, attn, attn_mate, out_weight, w_mate, (BF,))
    far_got = move_ahead(far)

    d_queries, d_pieces = backward(
        bounds, last_cols, rank_row, packed, after(queries, far), partial, last, out_weight,
        ks_col, qs_row, top, inv, 4 * mem,
    )
    d_pieces, w_got, far_got = lax.optimization_barrier((d_pieces, w_got, far_got))
    d_got = exchange(d_pieces, SECOND)

    to_ahead, to_behind, own = mixed_pieces(
        near_cols, attn, attn_mate, out_weight, w_mate, (BF, BF, F32), extra=(far_got,)
    )
    ahead_got, behind_got = move_ahead(to_ahead), move_behind(to_behind)

    def added(got):
        return f(got[0]) + f(got[1]) + f(got[2]) + f(got[3])

    def reduced(got, rows):
        sums = [added([part[k * rows : (k + 1) * rows] for part in got]) for k in range(4)]
        return added([sums[0]] + [move_first(sums[k].astype(BF), k) for k in (1, 2, 3)])

    d_out_weight = reduced(w_got, width)
    d_got, d_out_weight, ahead_got = lax.optimization_barrier((d_got, d_out_weight, ahead_got))
    d_kv = reduced(d_got, mem)
    mixed = (own + f(ahead_got) + f(behind_got)).astype(BF)
    return (mixed, d_queries, d_kv[:, :width], d_kv[:, width:], d_out_weight)


def solution(mesh):
    placed = (
        P("section", "mp"),
        P("section", "mp"),
        P("section", "mp"),
        P("mp", None),
        P("section", "mp"),
        P("section", None),
        P("section", None),
        P("section"),
    )
    return jax.shard_map(
        on_device,
        mesh=mesh,
        in_specs=placed,
        out_specs=(
            P("section", "mp"),
            P("section", "mp"),
            P("section", "mp"),
            P("section", "mp"),
            P("mp", "section"),
        ),
        check_vma=False,
    )
```

```python
import functools

import jax
import jax.numpy as jnp
from jax import lax
from jax.experimental import pallas as pl
from jax.experimental.pallas import tpu as pltpu
from jax.sharding import PartitionSpec as P

HD = 256
NEG = -1e30
BF = jnp.bfloat16
F32 = jnp.float32
NT = (((1,), (1,)), ((), ()))
NN = (((1,), (0,)), ((), ()))
TN = (((0,), (0,)), ((), ()))
VMEM_BYTES = 56 * 1024 * 1024


def moved(value, step):
    pairs = []
    for y in range(4):
        for z in range(4):
            for x in range(4):
                for c in range(2):
                    a, b, d, e = step(y, z, x, c)
                    pairs.append(
                        (
                            (y * 4 + z) * 8 + x * 2 + c,
                            ((a % 4) * 4 + b % 4) * 8 + (d % 4) * 2 + e % 2,
                        )
                    )
    return lax.ppermute(value, ("section", "mp"), pairs)


def move_core(value):
    return moved(value, lambda y, z, x, c: (y, z, x, c + 1))


def move_ahead(value):
    return moved(value, lambda y, z, x, c: (y, z, x + 1 - 2 * c, c))


def move_behind(value):
    return moved(value, lambda y, z, x, c: (y, z, x - 1 + 2 * c, c))


def move_first(value, by):
    return moved(value, lambda y, z, x, c: (y, z + by, x, c) if c == 0 else (y + by, z, x, c))


def lines(along_y):
    groups = []
    for x in range(4):
        for c in range(2):
            for o in range(4):
                at = [i * 4 + o if along_y[c] else o * 4 + i for i in range(4)]
                groups.append([p * 8 + x * 2 + c for p in at])
    return groups


FIRST = lines((False, True))
SECOND = lines((True, False))


def exchange(value, groups):
    return lax.all_to_all(value, ("section", "mp"), 0, 0, axis_index_groups=groups)


def dot(a, b, dims=NN):
    return lax.dot_general(a, b, dims, preferred_element_type=F32)


BLK = 256
FINE = 128
ROWS_IN = BLK + 16
ANY = pl.BlockSpec(memory_space=pl.ANY)
WHOLE = pl.BlockSpec(memory_space=pltpu.VMEM)
SCALARS = pl.BlockSpec(memory_space=pltpu.SMEM)
DMA = pltpu.SemaphoreType.DMA


def cut(ref, at, size):
    return ref.at[:, pl.ds(pl.multiple_of(at * size, size), size)]


def forward_kernel(
    bounds, secs, cols, rank_ref, src_in, q_in, ks_ref, qs_ref, g0, g1, g2, g3, g4, g5, g6, g7,
    packed_out, attn_out, top_ref, inv_ref, w_out,
    src, packed_ref, q_ref, attn_ref, attn_t, cot, weight, in_sem, q_sem, out_sem, cot_sem, w_sem,
):
    rows, width = q_ref.shape
    kv = packed_ref.shape[0]
    part = src_in.shape[1]
    loads = [pltpu.make_async_copy(src_in.at[t], src.at[t], in_sem.at[t]) for t in range(4)]
    q_load = pltpu.make_async_copy(q_in, q_ref, q_sem)
    for load in loads:
        load.start()
    q_load.start()
    cot_loads = []
    for n, g in enumerate((g0, g1, g2, g3, g4, g5, g6, g7)):
        for half in range(2):
            there = cot.at[2 * cols[n] + half]
            from_here = g.at[:, half * BLK : (half + 1) * BLK]
            cot_loads.append(pltpu.make_async_copy(from_here, there, cot_sem.at[2 * n + half]))
    packed_ref[...] = jnp.zeros_like(packed_ref)
    per = part // BLK
    for t in range(4 * per):
        if t % per == 0:
            loads[t // per].wait()
        start = pl.multiple_of(jnp.minimum(bounds[2 * t] // 16 * 16, kv - ROWS_IN), 16)
        at = rank_ref[:, t * BLK : (t + 1) * BLK]
        want = lax.broadcasted_iota(jnp.int32, (ROWS_IN, BLK), 0) + start
        pick = jnp.where(at == want, 1.0, 0.0).astype(BF)
        got = dot(pick, src[t // per, (t % per) * BLK : (t % per + 1) * BLK, :])
        packed_ref[pl.ds(start, ROWS_IN), :] += got.astype(BF)
    for load in cot_loads:
        load.start()
    packed_store = pltpu.make_async_copy(packed_ref, packed_out, out_sem.at[0])
    attn_store = pltpu.make_async_copy(attn_ref, attn_out, out_sem.at[1])
    stores = [pltpu.make_async_copy(weight.at[k], w_out.at[k], w_sem.at[k]) for k in range(4)]
    packed_store.start()
    q_load.wait()
    q_ref[...] = q_ref[...] * BF(HD**-0.5)
    n_heads = width // HD

    def weigh(h, k2):
        for k1 in range(4):
            lo = k1 * width + h * HD
            got = dot(attn_t[h * HD : (h + 1) * HD, :], cot[secs[k2 * 4 + k1]])
            weight[k2, lo : lo + HD, :] = got.astype(BF)

    def scores(h, b):
        lo = h * HD
        return dot(packed_ref[:, lo : lo + HD], q_ref[b : b + BLK, lo : lo + HD], NT)

    steps = [(h, b) for h in range(n_heads) for b in range(0, rows, BLK)]
    following = scores(*steps[0])
    for n, (h, b) in enumerate(steps):
        lo = h * HD
        if b == 0:
            v_t = packed_ref[:, width + lo : width + lo + HD].T
        s = following
        if n + 1 < len(steps):
            following = scores(*steps[n + 1])
        s = jnp.where(ks_ref[...] == qs_ref[:, b : b + BLK], s, NEG)
        top = jnp.max(s, axis=0, keepdims=True)
        e = jnp.exp(s - top)
        inv = 1.0 / jnp.sum(e, axis=0, keepdims=True)
        p = (e * inv).astype(BF)
        a_t = dot(v_t, p)
        attn_t[lo : lo + HD, b : b + BLK] = a_t.astype(BF)
        attn_ref[b : b + BLK, lo : lo + HD] = a_t.T.astype(BF)
        top_ref[h : h + 1, b : b + BLK] = top
        inv_ref[h : h + 1, b : b + BLK] = inv
        if h > 0:
            weigh(h - 1, b // BLK)
        if n == rows // BLK - 1:
            for load in cot_loads:
                load.wait()
    attn_store.start()
    for k2 in range(4):
        weigh(n_heads - 1, k2)
        stores[k2].start()
    for store in [packed_store, attn_store] + stores:
        store.wait()


def forward(bounds, secs, cols, rank_row, gathered_kv, queries, ks_col, qs_row, grads):
    rows, width = queries.shape
    kv = ks_col.shape[0]
    part = gathered_kv.shape[1]
    stat = jax.ShapeDtypeStruct((width // HD, rows), F32)
    return pl.pallas_call(
        forward_kernel,
        out_shape=(
            jax.ShapeDtypeStruct((kv, 2 * width), BF),
            jax.ShapeDtypeStruct((rows, width), BF),
            stat, stat,
            jax.ShapeDtypeStruct((4, 4 * width, BLK), BF),
        ),
        in_specs=[SCALARS] * 3 + [WHOLE] + [ANY] * 2 + [WHOLE] * 2 + [ANY] * 8,
        out_specs=(ANY, ANY, WHOLE, WHOLE, ANY),
        scratch_shapes=[
            pltpu.VMEM((4, part, 2 * width), BF),
            pltpu.VMEM((kv, 2 * width), BF),
            pltpu.VMEM((rows, width), BF),
            pltpu.VMEM((rows, width), BF),
            pltpu.VMEM((width, rows), BF),
            pltpu.VMEM((16, rows, BLK), BF),
            pltpu.VMEM((4, 4 * width, BLK), BF),
            DMA((4,)),
            DMA,
            DMA((2,)),
            DMA((16,)),
            DMA((4,)),
        ],
        compiler_params=pltpu.CompilerParams(vmem_limit_bytes=VMEM_BYTES),
        name="gather_forward",
    )(bounds, secs, cols, rank_row, gathered_kv, queries, ks_col, qs_row, *grads)


def backward_kernel(
    bounds, cols, rank_ref, packed_in, q_in, part_in, g0, g1, g2, g3, w_in, ks_ref, qs_ref, top_ref, inv_ref,
    dq_ref, out,
    packed_ref, q_ref, part_ref, cot, w_ref, da_ref, p_f, p_s, ds_s, dp_s, piece, in_sem, g_sem, w_sem, sem,
):
    rows, width = q_ref.shape
    kv = packed_ref.shape[0]
    scale = HD**-0.5
    n_heads = width // HD
    first = [
        pltpu.make_async_copy(packed_in, packed_ref, in_sem.at[0]),
        pltpu.make_async_copy(q_in, q_ref, in_sem.at[1]),
        pltpu.make_async_copy(part_in, part_ref, in_sem.at[2]),
    ]
    later = []
    for n, g in enumerate((g0, g1, g2, g3)):
        later.append(pltpu.make_async_copy(g, cot.at[:, n * width : (n + 1) * width], g_sem.at[n]))
        later.append(
            pltpu.make_async_copy(cut(w_in, cols[n], width), w_ref.at[:, n * width : (n + 1) * width], w_sem.at[n])
        )
    for load in first + later:
        load.start()
    first[0].wait()
    first[1].wait()
    q_ref[...] = q_ref[...] * BF(scale)

    def weights(h, b):
        lo = h * HD
        s = dot(packed_ref[:, lo : lo + HD], q_ref[b : b + BLK, lo : lo + HD], NT)
        s = jnp.where(ks_ref[...] == qs_ref[:, b : b + BLK], s, NEG)
        p = jnp.exp(s - top_ref[h : h + 1, b : b + BLK]) * inv_ref[h : h + 1, b : b + BLK]
        p_f[h, :, b : b + BLK] = p
        p_s[h, :, b : b + BLK] = p.astype(BF)

    for h in range(n_heads):
        for b in range(0, rows, BLK):
            weights(h, b)
    first[2].wait()
    for load in later:
        load.wait()
    for b in range(0, rows, BLK):
        rest = dot(cot[b : b + BLK, :], w_ref[...], NT)
        da_ref[b : b + BLK, :] = (part_ref[b : b + BLK, :] + rest).astype(BF)
    for h in range(n_heads):
        lo = h * HD
        k_t = packed_ref[:, lo : lo + HD].T
        v = packed_ref[:, width + lo : width + lo + HD]
        dp = dot(v, da_ref[0:BLK, lo : lo + HD], NT)
        for b in range(0, rows, BLK):
            following = dot(v, da_ref[b + BLK : b + 2 * BLK, lo : lo + HD], NT) if b + BLK < rows else None
            p = p_f[h, :, b : b + BLK]
            mean = jnp.sum(p * dp, axis=0, keepdims=True)
            ds = (p * (dp - mean)).astype(BF)
            ds_s[h, :, b : b + BLK] = ds
            dq_ref[b : b + BLK, lo : lo + HD] = (dot(k_t, ds) * scale).T.astype(BF)
            dp = following
        dp_s[:, lo : lo + HD] = dot(ds_s[h], q_ref[:, lo : lo + HD]).astype(BF)
        dp_s[:, width + lo : width + lo + HD] = dot(p_s[h], da_ref[:, lo : lo + HD]).astype(BF)
    part = out.shape[1]
    per = part // FINE
    stores = [pltpu.make_async_copy(piece.at[t], out.at[t], sem.at[t]) for t in range(4)]
    for n in range(4):
        for u in range(per):
            t = n * per + u
            start = pl.multiple_of(jnp.minimum(bounds[t] // FINE * FINE, kv - 2 * FINE), FINE)
            at = rank_ref[:, t * FINE : (t + 1) * FINE]
            have = lax.broadcasted_iota(jnp.int32, (2 * FINE, FINE), 0) + start
            put = jnp.where(at == have, 1.0, 0.0).astype(BF)
            piece[n, u * FINE : (u + 1) * FINE, :] = dot(put, dp_s[pl.ds(start, 2 * FINE), :], TN).astype(BF)
        stores[n].start()
    for store in stores:
        store.wait()


def backward(bounds, cols, rank_row, packed, queries, partial, grads, w, ks_col, qs_row, top, inv, part):
    rows, width = queries.shape
    kv = packed.shape[0]
    n_heads = width // HD
    return pl.pallas_call(
        backward_kernel,
        out_shape=(jax.ShapeDtypeStruct((rows, width), BF), jax.ShapeDtypeStruct((4, part, 2 * width), BF)),
        in_specs=[SCALARS] * 2 + [WHOLE] + [ANY] * 8 + [WHOLE] * 4,
        out_specs=(WHOLE, ANY),
        scratch_shapes=[
            pltpu.VMEM((kv, 2 * width), BF),
            pltpu.VMEM((rows, width), BF),
            pltpu.VMEM((rows, width), F32),
            pltpu.VMEM((rows, 4 * width), BF),
            pltpu.VMEM((width, 4 * width), BF),
            pltpu.VMEM((rows, width), BF),
            pltpu.VMEM((n_heads, kv, rows), F32),
            pltpu.VMEM((n_heads, kv, rows), BF),
            pltpu.VMEM((n_heads, kv, rows), BF),
            pltpu.VMEM((kv, 2 * width), BF),
            pltpu.VMEM((4, part, 2 * width), BF),
            DMA((3,)),
            DMA((4,)),
            DMA((4,)),
            DMA((4,)),
        ],
        compiler_params=pltpu.CompilerParams(vmem_limit_bytes=VMEM_BYTES),
        name="backward_scatter",
    )(bounds, cols, rank_row, packed, queries, partial, *grads, w, ks_col, qs_row, top, inv)


def d_attn_kernel(n_blocks, cols, *refs):
    grads, w_in, out_ref = refs[:n_blocks], refs[n_blocks], refs[n_blocks + 1]
    cot, w_ref, g_sem, w_sem = refs[n_blocks + 2 :]
    width = grads[0].shape[1]
    loads = []
    for n, g in enumerate(grads):
        loads.append(pltpu.make_async_copy(g, cot.at[:, n * width : (n + 1) * width], g_sem.at[n]))
        loads.append(
            pltpu.make_async_copy(cut(w_in, cols[n], width), w_ref.at[:, n * width : (n + 1) * width], w_sem.at[n])
        )
    for load in loads:
        load.start()
    for load in loads:
        load.wait()
    for b in range(0, out_ref.shape[0], BLK):
        out_ref[b : b + BLK, :] = dot(cot[b : b + BLK, :], w_ref[...], NT)


def d_attn_partial(cols, grads, w):
    rows, width = grads[0].shape
    heads = w.shape[0]
    n = len(grads)
    return pl.pallas_call(
        functools.partial(d_attn_kernel, n),
        out_shape=jax.ShapeDtypeStruct((rows, heads), F32),
        in_specs=[SCALARS] + [ANY] * (n + 1),
        out_specs=WHOLE,
        scratch_shapes=[
            pltpu.VMEM((rows, n * width), BF),
            pltpu.VMEM((heads, n * width), BF),
            DMA((n,)),
            DMA((n,)),
        ],
        compiler_params=pltpu.CompilerParams(vmem_limit_bytes=VMEM_BYTES),
        name="d_attn_partial",
    )(cols, *grads, w)


def mixed_kernel(n, add, cols, a_in, b_in, w_in, v_in, *refs):
    extra = refs[:add]
    outs = refs[add : add + n]
    a_ref, b_ref, w_ref, v_ref = refs[add + n : add + n + 4]
    bufs = refs[add + n + 4 : add + 2 * n + 4]
    sem, w_sem, v_sem, o_sem = refs[add + 2 * n + 4 :]
    width = w_ref.shape[2]
    loads = [pltpu.make_async_copy(a_in, a_ref, sem.at[0]), pltpu.make_async_copy(b_in, b_ref, sem.at[1])]
    w_loads, v_loads = [], []
    for i in range(n):
        w_loads.append(pltpu.make_async_copy(cut(w_in, cols[2 * i], width), w_ref.at[i], w_sem.at[i]))
        v_loads.append(pltpu.make_async_copy(cut(v_in, cols[2 * i + 1], width), v_ref.at[i], v_sem.at[i]))
    for load in [loads[0], w_loads[0], loads[1], v_loads[0]] + w_loads[1:] + v_loads[1:]:
        load.start()
    stores = [pltpu.make_async_copy(bufs[i], outs[i], o_sem.at[i]) for i in range(n)]
    for i in range(n):
        if i == 0:
            loads[0].wait()
            loads[1].wait()
        w_loads[i].wait()
        v_loads[i].wait()
        got = dot(a_ref[...], w_ref[i]) + dot(b_ref[...], v_ref[i])
        if i < add:
            got = got + extra[i][...].astype(F32)
        bufs[i][...] = got.astype(bufs[i].dtype)
        stores[i].start()
    for store in stores:
        store.wait()


def mixed_pieces(cols, attn, attn_mate, w, w_mate, kinds, extra=()):
    rows, heads = attn.shape
    width = 512
    n = len(kinds)
    add = len(extra)
    return pl.pallas_call(
        functools.partial(mixed_kernel, n, add),
        out_shape=tuple(jax.ShapeDtypeStruct((rows, width), kind) for kind in kinds),
        in_specs=[SCALARS] + [ANY] * 4 + [WHOLE] * add,
        out_specs=(ANY,) * n,
        scratch_shapes=[
            pltpu.VMEM((rows, heads), BF),
            pltpu.VMEM((rows, heads), BF),
            pltpu.VMEM((n, heads, width), BF),
            pltpu.VMEM((n, heads, width), BF),
        ]
        + [pltpu.VMEM((rows, width), kind) for kind in kinds]
        + [DMA((2,)), DMA((n,)), DMA((n,)), DMA((n,))],
        compiler_params=pltpu.CompilerParams(vmem_limit_bytes=VMEM_BYTES),
        name="mixed_pieces",
    )(cols, attn, attn_mate, w, w_mate, *extra)


def mate_kernel(core, w_in, out_ref, sem):
    width = 512
    copies = [
        pltpu.make_async_copy(cut(w_in, 2 * i + 1 - core[0], width), out_ref.at[:, i * width : (i + 1) * width], sem.at[i])
        for i in range(4)
    ]
    for copy in copies:
        copy.start()
    for copy in copies:
        copy.wait()


def columns_for_mate(core, w):
    heads, cols = w.shape
    return pl.pallas_call(
        mate_kernel,
        out_shape=jax.ShapeDtypeStruct((heads, cols // 2), w.dtype),
        in_specs=[SCALARS, ANY],
        out_specs=WHOLE,
        scratch_shapes=[DMA((4,))],
        compiler_params=pltpu.CompilerParams(vmem_limit_bytes=VMEM_BYTES),
        name="columns_for_mate",
    )(core, w)


def f(v):
    return v.astype(F32)


def after(value, *others):
    return lax.optimization_barrier((value,) + others)[0]


def on_device(queries, keys, values, out_weight, cotangent, pack, kv_seg, q_seg):
    p = lax.axis_index("section").astype(jnp.int32)
    m = lax.axis_index("mp").astype(jnp.int32)
    x, c = m // 2, m % 2
    ahead = 1 - 2 * c
    mem = keys.shape[0]
    width = queries.shape[1]
    first = jnp.where(c == 0, p % 4, p // 4)

    kv = jnp.concatenate((keys, values), axis=1)
    around = [move_first(kv, -k) for k in (1, 2, 3)]
    from_behind = move_ahead(cotangent)

    xs = jnp.stack((x, x, x - ahead, x + ahead, x + ahead, x - ahead, x + 2, x + 2)) % 4
    cols = 2 * xs + jnp.stack((c, 1 - c) * 4)
    d = jnp.arange(16, dtype=jnp.int32)
    to1 = (first + d) % 4
    sections = jnp.where(c == 0, d // 4 * 4 + to1, to1 * 4 + d // 4)

    def pair(to):
        to = to % 4
        return jnp.stack((2 * to + c, to))

    small = (
        sections, cols, cols[4:], pair(x + 2), jnp.concatenate((pair(x + ahead), pair(x - ahead), pair(x))),
    )
    w_send = columns_for_mate(c[None], out_weight)
    *around, from_behind, w_send, small = lax.optimization_barrier((*around, from_behind, w_send, small))
    sections, cols, last_cols, far_cols, near_cols = small

    near = jnp.concatenate([kv] + around, axis=0)
    gathered_kv = exchange(jnp.broadcast_to(near[None], (4,) + near.shape), SECOND)

    r, near = lax.optimization_barrier((pack[0], near))
    block = r // mem
    a1 = jnp.where(c == 0, block % 4, block // 4)
    a2 = jnp.where(c == 0, block // 4, block % 4)
    idx = (a2 * 4 + (a1 - first) % 4) * mem + r % mem
    rank = jnp.sum((idx[None, :] < idx[:, None]).astype(jnp.int32), axis=1)
    places = jnp.arange(16 * mem, dtype=jnp.int32)
    rank_row = jnp.max(jnp.where(idx[:, None] == places[None, :], rank[:, None], -1), axis=0)[None, :]
    order = jnp.arange(r.shape[0], dtype=jnp.int32)
    seg = jnp.sum(jnp.where(rank[:, None] == order[None, :], kv_seg[0][:, None], 0), axis=0)
    starts = jnp.arange(0, 16 * mem, FINE, dtype=jnp.int32)
    bounds = jnp.sum((idx[None, :] < starts[:, None]).astype(jnp.int32), axis=1)
    ks_col, qs_row = seg[:, None], q_seg[None, :]

    from_far, from_ahead = move_ahead(from_behind), move_behind(after(cotangent, near))
    own_mate = move_core(after(cotangent, near))
    behind_mate = move_core(from_behind)
    grads = (cotangent, own_mate, from_behind, behind_mate)
    partial = d_attn_partial(cols[:4], grads, out_weight)
    bounds, ks_col, rank_row, partial, from_ahead, from_far = lax.optimization_barrier(
        (bounds, ks_col, rank_row, partial, from_ahead, from_far)
    )
    bounds, ahead_mate, far_mate, w_mate = lax.optimization_barrier(
        (bounds, move_core(from_ahead), move_core(from_far), move_core(after(w_send, near)))
    )
    last = (from_ahead, ahead_mate, from_far, far_mate)

    packed, attn, top, inv, pieces = forward(
        bounds, sections, cols, rank_row, gathered_kv, queries, ks_col, qs_row, grads + last
    )
    attn_mate = move_core(attn)
    w_got = exchange(pieces, SECOND)

    (far,) = mixed_pieces(far_cols, attn, attn_mate, out_weight, w_mate, (BF,))
    far_got = move_ahead(far)

    d_queries, d_pieces = backward(
        bounds, last_cols, rank_row, packed, after(queries, far), partial, last, out_weight,
        ks_col, qs_row, top, inv, 4 * mem,
    )
    d_pieces, far_got = lax.optimization_barrier((d_pieces, far_got))
    d_got = exchange(d_pieces, SECOND)

    to_ahead, to_behind, own = mixed_pieces(
        near_cols, attn, attn_mate, out_weight, w_mate, (BF, BF, F32), extra=(far_got,)
    )
    ahead_got, behind_got = move_ahead(to_ahead), move_behind(to_behind)
    w_got, own = lax.optimization_barrier((w_got, own))

    def added(got):
        return f(got[0]) + f(got[1]) + f(got[2]) + f(got[3])

    def to_send(got, rows):
        return [added([part[k * rows : (k + 1) * rows] for part in got]) for k in range(4)]

    w_own, *w_sums = to_send(w_got, width)
    w_back = [move_first(v.astype(BF), k) for k, v in zip((1, 2, 3), w_sums)]
    d_got, w_back, ahead_got = lax.optimization_barrier((d_got, w_back, ahead_got))
    d_own, *d_sums = to_send(d_got, mem)
    d_back = [move_first(v.astype(BF), k) for k, v in zip((1, 2, 3), d_sums)]
    d_out_weight = added([w_own] + w_back)
    d_keys = added([v[:, :width] for v in [d_own] + d_back])
    d_values = added([v[:, width:] for v in [d_own] + d_back])
    mixed = (own + f(ahead_got) + f(behind_got)).astype(BF)
    return (mixed, d_queries, d_keys, d_values, d_out_weight)


def solution(mesh):
    placed = (
        P("section", "mp"),
        P("section", "mp"),
        P("section", "mp"),
        P("mp", None),
        P("section", "mp"),
        P("section", None),
        P("section", None),
        P("section"),
    )
    return jax.shard_map(
        on_device,
        mesh=mesh,
        in_specs=placed,
        out_specs=(
            P("section", "mp"),
            P("section", "mp"),
            P("section", "mp"),
            P("section", "mp"),
            P("mp", "section"),
        ),
        check_vma=False,
    )
```

```python
import functools

import jax
import jax.numpy as jnp
from jax import lax
from jax.experimental import pallas as pl
from jax.experimental.pallas import tpu as pltpu
from jax.sharding import PartitionSpec as P

HD = 256
NEG = -1e30
BF = jnp.bfloat16
F32 = jnp.float32
NT = (((1,), (1,)), ((), ()))
NN = (((1,), (0,)), ((), ()))
TN = (((0,), (0,)), ((), ()))
VMEM_BYTES = 56 * 1024 * 1024


def moved(value, step):
    pairs = []
    for y in range(4):
        for z in range(4):
            for x in range(4):
                for c in range(2):
                    a, b, d, e = step(y, z, x, c)
                    pairs.append(
                        (
                            (y * 4 + z) * 8 + x * 2 + c,
                            ((a % 4) * 4 + b % 4) * 8 + (d % 4) * 2 + e % 2,
                        )
                    )
    return lax.ppermute(value, ("section", "mp"), pairs)


def move_core(value):
    return moved(value, lambda y, z, x, c: (y, z, x, c + 1))


def move_ahead(value):
    return moved(value, lambda y, z, x, c: (y, z, x + 1 - 2 * c, c))


def move_behind(value):
    return moved(value, lambda y, z, x, c: (y, z, x - 1 + 2 * c, c))


def move_first(value, by):
    return moved(value, lambda y, z, x, c: (y, z + by, x, c) if c == 0 else (y + by, z, x, c))


def lines(along_y):
    groups = []
    for x in range(4):
        for c in range(2):
            for o in range(4):
                at = [i * 4 + o if along_y[c] else o * 4 + i for i in range(4)]
                groups.append([p * 8 + x * 2 + c for p in at])
    return groups


FIRST = lines((False, True))
SECOND = lines((True, False))


def exchange(value, groups):
    return lax.all_to_all(value, ("section", "mp"), 0, 0, axis_index_groups=groups)


def dot(a, b, dims=NN):
    return lax.dot_general(a, b, dims, preferred_element_type=F32)


BLK = 256
FINE = 128
ROWS_IN = BLK + 16
ANY = pl.BlockSpec(memory_space=pl.ANY)
WHOLE = pl.BlockSpec(memory_space=pltpu.VMEM)
SCALARS = pl.BlockSpec(memory_space=pltpu.SMEM)
DMA = pltpu.SemaphoreType.DMA


def cut(ref, at, size):
    return ref.at[:, pl.ds(pl.multiple_of(at * size, size), size)]


def forward_kernel(
    bounds, secs, cols, rank_ref, src_in, q_in, ks_ref, qs_ref, g0, g1, g2, g3, g4, g5, g6, g7,
    packed_out, attn_out, top_ref, inv_ref, w_out,
    src, packed_ref, q_ref, attn_ref, attn_t, cot, weight, in_sem, q_sem, out_sem, cot_sem, w_sem,
):
    rows, width = q_ref.shape
    kv = packed_ref.shape[0]
    part = src_in.shape[1]
    loads = [pltpu.make_async_copy(src_in.at[t], src.at[t], in_sem.at[t]) for t in range(4)]
    q_load = pltpu.make_async_copy(q_in, q_ref, q_sem)
    for load in loads:
        load.start()
    q_load.start()
    cot_loads = []
    for n, g in enumerate((g0, g1, g2, g3, g4, g5, g6, g7)):
        for half in range(2):
            there = cot.at[2 * cols[n] + half]
            from_here = g.at[:, half * BLK : (half + 1) * BLK]
            cot_loads.append(pltpu.make_async_copy(from_here, there, cot_sem.at[2 * n + half]))
    packed_ref[...] = jnp.zeros_like(packed_ref)
    per = part // BLK
    for t in range(4 * per):
        if t % per == 0:
            loads[t // per].wait()
        start = pl.multiple_of(jnp.minimum(bounds[2 * t] // 16 * 16, kv - ROWS_IN), 16)
        at = rank_ref[:, t * BLK : (t + 1) * BLK]
        want = lax.broadcasted_iota(jnp.int32, (ROWS_IN, BLK), 0) + start
        pick = jnp.where(at == want, 1.0, 0.0).astype(BF)
        got = dot(pick, src[t // per, (t % per) * BLK : (t % per + 1) * BLK, :])
        packed_ref[pl.ds(start, ROWS_IN), :] += got.astype(BF)
    for load in cot_loads:
        load.start()
    packed_store = pltpu.make_async_copy(packed_ref, packed_out, out_sem.at[0])
    attn_store = pltpu.make_async_copy(attn_ref, attn_out, out_sem.at[1])
    stores = [pltpu.make_async_copy(weight.at[k], w_out.at[k], w_sem.at[k]) for k in range(4)]
    packed_store.start()
    q_load.wait()
    q_ref[...] = q_ref[...] * BF(HD**-0.5)
    n_heads = width // HD

    def weigh(h, k2):
        for k1 in range(4):
            lo = k1 * width + h * HD
            got = dot(attn_t[h * HD : (h + 1) * HD, :], cot[secs[k2 * 4 + k1]])
            weight[k2, lo : lo + HD, :] = got.astype(BF)

    def scores(h, b):
        lo = h * HD
        return dot(packed_ref[:, lo : lo + HD], q_ref[b : b + BLK, lo : lo + HD], NT)

    steps = [(h, b) for h in range(n_heads) for b in range(0, rows, BLK)]
    following = scores(*steps[0])
    for n, (h, b) in enumerate(steps):
        lo = h * HD
        if b == 0:
            v_t = packed_ref[:, width + lo : width + lo + HD].T
        s = following
        if n + 1 < len(steps):
            following = scores(*steps[n + 1])
        s = jnp.where(ks_ref[...] == qs_ref[:, b : b + BLK], s, NEG)
        top = jnp.max(s, axis=0, keepdims=True)
        e = jnp.exp(s - top)
        inv = 1.0 / jnp.sum(e, axis=0, keepdims=True)
        p = (e * inv).astype(BF)
        a_t = dot(v_t, p)
        attn_t[lo : lo + HD, b : b + BLK] = a_t.astype(BF)
        attn_ref[b : b + BLK, lo : lo + HD] = a_t.T.astype(BF)
        top_ref[h : h + 1, b : b + BLK] = top
        inv_ref[h : h + 1, b : b + BLK] = inv
        if h > 0:
            weigh(h - 1, b // BLK)
        if n == rows // BLK - 1:
            for load in cot_loads:
                load.wait()
    attn_store.start()
    for k2 in range(4):
        weigh(n_heads - 1, k2)
        stores[k2].start()
    for store in [packed_store, attn_store] + stores:
        store.wait()


def forward(bounds, secs, cols, rank_row, gathered_kv, queries, ks_col, qs_row, grads):
    rows, width = queries.shape
    kv = ks_col.shape[0]
    part = gathered_kv.shape[1]
    stat = jax.ShapeDtypeStruct((width // HD, rows), F32)
    return pl.pallas_call(
        forward_kernel,
        out_shape=(
            jax.ShapeDtypeStruct((kv, 2 * width), BF),
            jax.ShapeDtypeStruct((rows, width), BF),
            stat, stat,
            jax.ShapeDtypeStruct((4, 4 * width, BLK), BF),
        ),
        in_specs=[SCALARS] * 3 + [WHOLE] + [ANY] * 2 + [WHOLE] * 2 + [ANY] * 8,
        out_specs=(ANY, ANY, WHOLE, WHOLE, ANY),
        scratch_shapes=[
            pltpu.VMEM((4, part, 2 * width), BF),
            pltpu.VMEM((kv, 2 * width), BF),
            pltpu.VMEM((rows, width), BF),
            pltpu.VMEM((rows, width), BF),
            pltpu.VMEM((width, rows), BF),
            pltpu.VMEM((16, rows, BLK), BF),
            pltpu.VMEM((4, 4 * width, BLK), BF),
            DMA((4,)),
            DMA,
            DMA((2,)),
            DMA((16,)),
            DMA((4,)),
        ],
        compiler_params=pltpu.CompilerParams(vmem_limit_bytes=VMEM_BYTES),
        name="gather_forward",
    )(bounds, secs, cols, rank_row, gathered_kv, queries, ks_col, qs_row, *grads)


def backward_kernel(
    bounds, cols, rank_ref, packed_in, q_in, part_in, g0, g1, g2, g3, w_in, ks_ref, qs_ref, top_ref, inv_ref,
    dq_ref, out,
    packed_ref, q_ref, part_ref, cot, w_ref, da_ref, p_f, p_s, ds_s, dp_s, piece, in_sem, g_sem, w_sem, sem,
):
    rows, width = q_ref.shape
    kv = packed_ref.shape[0]
    scale = HD**-0.5
    n_heads = width // HD
    first = [
        pltpu.make_async_copy(packed_in, packed_ref, in_sem.at[0]),
        pltpu.make_async_copy(q_in, q_ref, in_sem.at[1]),
        pltpu.make_async_copy(part_in, part_ref, in_sem.at[2]),
    ]
    later = []
    for n, g in enumerate((g0, g1, g2, g3)):
        later.append(pltpu.make_async_copy(g, cot.at[:, n * width : (n + 1) * width], g_sem.at[n]))
        later.append(
            pltpu.make_async_copy(cut(w_in, cols[n], width), w_ref.at[:, n * width : (n + 1) * width], w_sem.at[n])
        )
    for load in first + later:
        load.start()
    first[0].wait()
    first[1].wait()
    q_ref[...] = q_ref[...] * BF(scale)

    def weights(h, b):
        lo = h * HD
        s = dot(packed_ref[:, lo : lo + HD], q_ref[b : b + BLK, lo : lo + HD], NT)
        s = jnp.where(ks_ref[...] == qs_ref[:, b : b + BLK], s, NEG)
        p = jnp.exp(s - top_ref[h : h + 1, b : b + BLK]) * inv_ref[h : h + 1, b : b + BLK]
        p_f[h, :, b : b + BLK] = p
        p_s[h, :, b : b + BLK] = p.astype(BF)

    for h in range(n_heads):
        for b in range(0, rows, BLK):
            weights(h, b)
    first[2].wait()
    for load in later:
        load.wait()
    for b in range(0, rows, BLK):
        rest = dot(cot[b : b + BLK, :], w_ref[...], NT)
        da_ref[b : b + BLK, :] = (part_ref[b : b + BLK, :] + rest).astype(BF)
    for h in range(n_heads):
        lo = h * HD
        k_t = packed_ref[:, lo : lo + HD].T
        v = packed_ref[:, width + lo : width + lo + HD]
        dp = dot(v, da_ref[0:BLK, lo : lo + HD], NT)
        for b in range(0, rows, BLK):
            following = dot(v, da_ref[b + BLK : b + 2 * BLK, lo : lo + HD], NT) if b + BLK < rows else None
            p = p_f[h, :, b : b + BLK]
            mean = jnp.sum(p * dp, axis=0, keepdims=True)
            ds = (p * (dp - mean)).astype(BF)
            ds_s[h, :, b : b + BLK] = ds
            dq_ref[b : b + BLK, lo : lo + HD] = (dot(k_t, ds) * scale).T.astype(BF)
            dp = following
        dp_s[:, lo : lo + HD] = dot(ds_s[h], q_ref[:, lo : lo + HD]).astype(BF)
        dp_s[:, width + lo : width + lo + HD] = dot(p_s[h], da_ref[:, lo : lo + HD]).astype(BF)
    part = out.shape[1]
    per = part // FINE
    stores = [pltpu.make_async_copy(piece.at[t], out.at[t], sem.at[t]) for t in range(4)]
    for n in range(4):
        for u in range(per):
            t = n * per + u
            start = pl.multiple_of(jnp.minimum(bounds[t] // FINE * FINE, kv - 2 * FINE), FINE)
            at = rank_ref[:, t * FINE : (t + 1) * FINE]
            have = lax.broadcasted_iota(jnp.int32, (2 * FINE, FINE), 0) + start
            put = jnp.where(at == have, 1.0, 0.0).astype(BF)
            piece[n, u * FINE : (u + 1) * FINE, :] = dot(put, dp_s[pl.ds(start, 2 * FINE), :], TN).astype(BF)
        stores[n].start()
    for store in stores:
        store.wait()


def backward(bounds, cols, rank_row, packed, queries, partial, grads, w, ks_col, qs_row, top, inv, part):
    rows, width = queries.shape
    kv = packed.shape[0]
    n_heads = width // HD
    return pl.pallas_call(
        backward_kernel,
        out_shape=(jax.ShapeDtypeStruct((rows, width), BF), jax.ShapeDtypeStruct((4, part, 2 * width), BF)),
        in_specs=[SCALARS] * 2 + [WHOLE] + [ANY] * 8 + [WHOLE] * 4,
        out_specs=(WHOLE, ANY),
        scratch_shapes=[
            pltpu.VMEM((kv, 2 * width), BF),
            pltpu.VMEM((rows, width), BF),
            pltpu.VMEM((rows, width), F32),
            pltpu.VMEM((rows, 4 * width), BF),
            pltpu.VMEM((width, 4 * width), BF),
            pltpu.VMEM((rows, width), BF),
            pltpu.VMEM((n_heads, kv, rows), F32),
            pltpu.VMEM((n_heads, kv, rows), BF),
            pltpu.VMEM((n_heads, kv, rows), BF),
            pltpu.VMEM((kv, 2 * width), BF),
            pltpu.VMEM((4, part, 2 * width), BF),
            DMA((3,)),
            DMA((4,)),
            DMA((4,)),
            DMA((4,)),
        ],
        compiler_params=pltpu.CompilerParams(vmem_limit_bytes=VMEM_BYTES),
        name="backward_scatter",
    )(bounds, cols, rank_row, packed, queries, partial, *grads, w, ks_col, qs_row, top, inv)


def d_attn_kernel(n_blocks, cols, *refs):
    grads, w_in, out_ref = refs[:n_blocks], refs[n_blocks], refs[n_blocks + 1]
    cot, w_ref, g_sem, w_sem = refs[n_blocks + 2 :]
    width = grads[0].shape[1]
    loads = []
    for n, g in enumerate(grads):
        loads.append(pltpu.make_async_copy(g, cot.at[:, n * width : (n + 1) * width], g_sem.at[n]))
        loads.append(
            pltpu.make_async_copy(cut(w_in, cols[n], width), w_ref.at[:, n * width : (n + 1) * width], w_sem.at[n])
        )
    for load in loads:
        load.start()
    for load in loads:
        load.wait()
    for b in range(0, out_ref.shape[0], BLK):
        out_ref[b : b + BLK, :] = dot(cot[b : b + BLK, :], w_ref[...], NT)


def d_attn_partial(cols, grads, w):
    rows, width = grads[0].shape
    heads = w.shape[0]
    n = len(grads)
    return pl.pallas_call(
        functools.partial(d_attn_kernel, n),
        out_shape=jax.ShapeDtypeStruct((rows, heads), F32),
        in_specs=[SCALARS] + [ANY] * (n + 1),
        out_specs=WHOLE,
        scratch_shapes=[
            pltpu.VMEM((rows, n * width), BF),
            pltpu.VMEM((heads, n * width), BF),
            DMA((n,)),
            DMA((n,)),
        ],
        compiler_params=pltpu.CompilerParams(vmem_limit_bytes=VMEM_BYTES),
        name="d_attn_partial",
    )(cols, *grads, w)


def mixed_kernel(n, add, cols, a_in, b_in, w_in, v_in, *refs):
    extra = refs[:add]
    outs = refs[add : add + n]
    a_ref, b_ref, w_ref, v_ref = refs[add + n : add + n + 4]
    bufs = refs[add + n + 4 : add + 2 * n + 4]
    sem, w_sem, v_sem, o_sem = refs[add + 2 * n + 4 :]
    width = w_ref.shape[2]
    loads = [pltpu.make_async_copy(a_in, a_ref, sem.at[0]), pltpu.make_async_copy(b_in, b_ref, sem.at[1])]
    w_loads, v_loads = [], []
    for i in range(n):
        w_loads.append(pltpu.make_async_copy(cut(w_in, cols[2 * i], width), w_ref.at[i], w_sem.at[i]))
        v_loads.append(pltpu.make_async_copy(cut(v_in, cols[2 * i + 1], width), v_ref.at[i], v_sem.at[i]))
    for load in [loads[0], w_loads[0], loads[1], v_loads[0]] + w_loads[1:] + v_loads[1:]:
        load.start()
    stores = [pltpu.make_async_copy(bufs[i], outs[i], o_sem.at[i]) for i in range(n)]
    for i in range(n):
        if i == 0:
            loads[0].wait()
            loads[1].wait()
        w_loads[i].wait()
        v_loads[i].wait()
        got = dot(a_ref[...], w_ref[i]) + dot(b_ref[...], v_ref[i])
        if i < add:
            got = got + extra[i][...].astype(F32)
        bufs[i][...] = got.astype(bufs[i].dtype)
        stores[i].start()
    for store in stores:
        store.wait()


def mixed_pieces(cols, attn, attn_mate, w, w_mate, kinds, extra=()):
    rows, heads = attn.shape
    width = 512
    n = len(kinds)
    add = len(extra)
    return pl.pallas_call(
        functools.partial(mixed_kernel, n, add),
        out_shape=tuple(jax.ShapeDtypeStruct((rows, width), kind) for kind in kinds),
        in_specs=[SCALARS] + [ANY] * 4 + [WHOLE] * add,
        out_specs=(ANY,) * n,
        scratch_shapes=[
            pltpu.VMEM((rows, heads), BF),
            pltpu.VMEM((rows, heads), BF),
            pltpu.VMEM((n, heads, width), BF),
            pltpu.VMEM((n, heads, width), BF),
        ]
        + [pltpu.VMEM((rows, width), kind) for kind in kinds]
        + [DMA((2,)), DMA((n,)), DMA((n,)), DMA((n,))],
        compiler_params=pltpu.CompilerParams(vmem_limit_bytes=VMEM_BYTES),
        name="mixed_pieces",
    )(cols, attn, attn_mate, w, w_mate, *extra)


def mate_kernel(core, w_in, out_ref, sem):
    width = 512
    copies = [
        pltpu.make_async_copy(cut(w_in, 2 * i + 1 - core[0], width), out_ref.at[:, i * width : (i + 1) * width], sem.at[i])
        for i in range(4)
    ]
    for copy in copies:
        copy.start()
    for copy in copies:
        copy.wait()


def columns_for_mate(core, w):
    heads, cols = w.shape
    return pl.pallas_call(
        mate_kernel,
        out_shape=jax.ShapeDtypeStruct((heads, cols // 2), w.dtype),
        in_specs=[SCALARS, ANY],
        out_specs=WHOLE,
        scratch_shapes=[DMA((4,))],
        compiler_params=pltpu.CompilerParams(vmem_limit_bytes=VMEM_BYTES),
        name="columns_for_mate",
    )(core, w)


def f(v):
    return v.astype(F32)


def after(value, *others):
    return lax.optimization_barrier((value,) + others)[0]


def on_device(queries, keys, values, out_weight, cotangent, pack, kv_seg, q_seg):
    p = lax.axis_index("section").astype(jnp.int32)
    m = lax.axis_index("mp").astype(jnp.int32)
    x, c = m // 2, m % 2
    ahead = 1 - 2 * c
    mem = keys.shape[0]
    width = queries.shape[1]
    first = jnp.where(c == 0, p % 4, p // 4)

    kv = jnp.concatenate((keys, values), axis=1)
    around = [move_first(kv, -k) for k in (1, 2, 3)]
    from_behind = move_ahead(cotangent)

    xs = jnp.stack((x, x, x - ahead, x + ahead, x + ahead, x - ahead, x + 2, x + 2)) % 4
    cols = 2 * xs + jnp.stack((c, 1 - c) * 4)
    d = jnp.arange(16, dtype=jnp.int32)
    to1 = (first + d) % 4
    sections = jnp.where(c == 0, d // 4 * 4 + to1, to1 * 4 + d // 4)

    def pair(to):
        to = to % 4
        return jnp.stack((2 * to + c, to))

    small = (
        sections, cols, cols[4:], pair(x + 2), pair(x + ahead), jnp.concatenate((pair(x - ahead), pair(x))),
    )
    w_send = columns_for_mate(c[None], out_weight)
    *around, from_behind, w_send, small = lax.optimization_barrier((*around, from_behind, w_send, small))
    sections, cols, last_cols, far_cols, ahead_cols, near_cols = small

    near = jnp.concatenate([kv] + around, axis=0)
    gathered_kv = exchange(jnp.broadcast_to(near[None], (4,) + near.shape), SECOND)

    r, near = lax.optimization_barrier((pack[0], near))
    block = r // mem
    a1 = jnp.where(c == 0, block % 4, block // 4)
    a2 = jnp.where(c == 0, block // 4, block % 4)
    idx = (a2 * 4 + (a1 - first) % 4) * mem + r % mem
    rank = jnp.sum((idx[None, :] < idx[:, None]).astype(jnp.int32), axis=1)
    places = jnp.arange(16 * mem, dtype=jnp.int32)
    rank_row = jnp.max(jnp.where(idx[:, None] == places[None, :], rank[:, None], -1), axis=0)[None, :]
    order = jnp.arange(r.shape[0], dtype=jnp.int32)
    seg = jnp.sum(jnp.where(rank[:, None] == order[None, :], kv_seg[0][:, None], 0), axis=0)
    starts = jnp.arange(0, 16 * mem, FINE, dtype=jnp.int32)
    bounds = jnp.sum((idx[None, :] < starts[:, None]).astype(jnp.int32), axis=1)
    ks_col, qs_row = seg[:, None], q_seg[None, :]

    from_far, from_ahead = move_ahead(from_behind), move_behind(after(cotangent, near))
    own_mate = move_core(after(cotangent, near))
    behind_mate = move_core(from_behind)
    grads = (cotangent, own_mate, from_behind, behind_mate)
    partial = d_attn_partial(cols[:4], grads, out_weight)
    bounds, ks_col, rank_row, partial, from_ahead, from_far = lax.optimization_barrier(
        (bounds, ks_col, rank_row, partial, from_ahead, from_far)
    )
    bounds, ahead_mate, far_mate, w_mate = lax.optimization_barrier(
        (bounds, move_core(from_ahead), move_core(from_far), move_core(after(w_send, near)))
    )
    last = (from_ahead, ahead_mate, from_far, far_mate)

    packed, attn, top, inv, pieces = forward(
        bounds, sections, cols, rank_row, gathered_kv, queries, ks_col, qs_row, grads + last
    )
    attn_mate = move_core(attn)
    w_got = exchange(pieces, SECOND)

    (far,) = mixed_pieces(far_cols, attn, attn_mate, out_weight, w_mate, (BF,))
    far_got = move_ahead(far)

    d_queries, d_pieces = backward(
        bounds, last_cols, rank_row, packed, after(queries, far), partial, last, out_weight,
        ks_col, qs_row, top, inv, 4 * mem,
    )
    d_pieces, far_got = lax.optimization_barrier((d_pieces, far_got))
    d_got = exchange(d_pieces, SECOND)

    (to_ahead,) = mixed_pieces(ahead_cols, attn, attn_mate, out_weight, w_mate, (BF,), extra=(far_got,))
    ahead_got = move_ahead(to_ahead)
    to_behind, own = mixed_pieces(near_cols, attn, after(attn_mate, to_ahead), out_weight, w_mate, (BF, F32))
    behind_got = move_behind(to_behind)
    w_got, own = lax.optimization_barrier((w_got, own))

    def added(got):
        return f(got[0]) + f(got[1]) + f(got[2]) + f(got[3])

    def to_send(got, rows):
        return [added([part[k * rows : (k + 1) * rows] for part in got]) for k in range(4)]

    w_own, *w_sums = to_send(w_got, width)
    w_back = [move_first(v.astype(BF), k) for k, v in zip((1, 2, 3), w_sums)]
    d_got, w_back, ahead_got = lax.optimization_barrier((d_got, w_back, ahead_got))
    d_own, *d_sums = to_send(d_got, mem)
    d_back = [move_first(v.astype(BF), k) for k, v in zip((1, 2, 3), d_sums)]
    d_out_weight = added([w_own] + w_back)
    d_keys = added([v[:, :width] for v in [d_own] + d_back])
    d_values = added([v[:, width:] for v in [d_own] + d_back])
    mixed = (own + f(ahead_got) + f(behind_got)).astype(BF)
    return (mixed, d_queries, d_keys, d_values, d_out_weight)


def solution(mesh):
    placed = (
        P("section", "mp"),
        P("section", "mp"),
        P("section", "mp"),
        P("mp", None),
        P("section", "mp"),
        P("section", None),
        P("section", None),
        P("section"),
    )
    return jax.shard_map(
        on_device,
        mesh=mesh,
        in_specs=placed,
        out_specs=(
            P("section", "mp"),
            P("section", "mp"),
            P("section", "mp"),
            P("section", "mp"),
            P("mp", "section"),
        ),
        check_vma=False,
    )
```

```python
import functools

import jax
import jax.numpy as jnp
from jax import lax
from jax.experimental import pallas as pl
from jax.experimental.pallas import tpu as pltpu
from jax.sharding import PartitionSpec as P

HD = 256
NEG = -1e30
BF = jnp.bfloat16
F32 = jnp.float32
NT = (((1,), (1,)), ((), ()))
NN = (((1,), (0,)), ((), ()))
TN = (((0,), (0,)), ((), ()))
VMEM_BYTES = 56 * 1024 * 1024


def moved(value, step):
    pairs = []
    for y in range(4):
        for z in range(4):
            for x in range(4):
                for c in range(2):
                    a, b, d, e = step(y, z, x, c)
                    pairs.append(
                        (
                            (y * 4 + z) * 8 + x * 2 + c,
                            ((a % 4) * 4 + b % 4) * 8 + (d % 4) * 2 + e % 2,
                        )
                    )
    return lax.ppermute(value, ("section", "mp"), pairs)


def move_core(value):
    return moved(value, lambda y, z, x, c: (y, z, x, c + 1))


def move_ahead(value):
    return moved(value, lambda y, z, x, c: (y, z, x + 1 - 2 * c, c))


def move_behind(value):
    return moved(value, lambda y, z, x, c: (y, z, x - 1 + 2 * c, c))


def move_first(value, by):
    return moved(value, lambda y, z, x, c: (y, z + by, x, c) if c == 0 else (y + by, z, x, c))


def lines(along_y):
    groups = []
    for x in range(4):
        for c in range(2):
            for o in range(4):
                at = [i * 4 + o if along_y[c] else o * 4 + i for i in range(4)]
                groups.append([p * 8 + x * 2 + c for p in at])
    return groups


FIRST = lines((False, True))
SECOND = lines((True, False))


def exchange(value, groups):
    return lax.all_to_all(value, ("section", "mp"), 0, 0, axis_index_groups=groups)


def dot(a, b, dims=NN):
    return lax.dot_general(a, b, dims, preferred_element_type=F32)


BLK = 256
FINE = 128
ROWS_IN = BLK + 16
ANY = pl.BlockSpec(memory_space=pl.ANY)
WHOLE = pl.BlockSpec(memory_space=pltpu.VMEM)
SCALARS = pl.BlockSpec(memory_space=pltpu.SMEM)
DMA = pltpu.SemaphoreType.DMA


def cut(ref, at, size):
    return ref.at[:, pl.ds(pl.multiple_of(at * size, size), size)]


def forward_kernel(
    bounds, secs, cols, rank_ref, src_in, q_in, ks_ref, qs_ref, g0, g1, g2, g3, g4, g5, g6, g7,
    packed_out, attn_out, top_ref, inv_ref, w_out,
    src, packed_ref, q_ref, attn_ref, attn_t, cot, weight, in_sem, q_sem, out_sem, cot_sem, w_sem,
):
    rows, width = q_ref.shape
    kv = packed_ref.shape[0]
    part = src_in.shape[1]
    loads = [pltpu.make_async_copy(src_in.at[t], src.at[t], in_sem.at[t]) for t in range(4)]
    q_load = pltpu.make_async_copy(q_in, q_ref, q_sem)
    for load in loads:
        load.start()
    q_load.start()
    cot_loads = []
    for n, g in enumerate((g0, g1, g2, g3, g4, g5, g6, g7)):
        for half in range(2):
            there = cot.at[2 * cols[n] + half]
            from_here = g.at[:, half * BLK : (half + 1) * BLK]
            cot_loads.append(pltpu.make_async_copy(from_here, there, cot_sem.at[2 * n + half]))
    packed_ref[...] = jnp.zeros_like(packed_ref)
    per = part // BLK
    for t in range(4 * per):
        if t % per == 0:
            loads[t // per].wait()
        start = pl.multiple_of(jnp.minimum(bounds[2 * t] // 16 * 16, kv - ROWS_IN), 16)
        at = rank_ref[:, t * BLK : (t + 1) * BLK]
        want = lax.broadcasted_iota(jnp.int32, (ROWS_IN, BLK), 0) + start
        pick = jnp.where(at == want, 1.0, 0.0).astype(BF)
        got = dot(pick, src[t // per, (t % per) * BLK : (t % per + 1) * BLK, :])
        packed_ref[pl.ds(start, ROWS_IN), :] += got.astype(BF)
    for load in cot_loads:
        load.start()
    packed_store = pltpu.make_async_copy(packed_ref, packed_out, out_sem.at[0])
    attn_store = pltpu.make_async_copy(attn_ref, attn_out, out_sem.at[1])
    stores = [pltpu.make_async_copy(weight.at[k], w_out.at[k], w_sem.at[k]) for k in range(4)]
    packed_store.start()
    q_load.wait()
    q_ref[...] = q_ref[...] * BF(HD**-0.5)
    n_heads = width // HD

    def weigh(h, k2):
        for k1 in range(4):
            lo = k1 * width + h * HD
            got = dot(attn_t[h * HD : (h + 1) * HD, :], cot[secs[k2 * 4 + k1]])
            weight[k2, lo : lo + HD, :] = got.astype(BF)

    def scores(h, b):
        lo = h * HD
        return dot(packed_ref[:, lo : lo + HD], q_ref[b : b + BLK, lo : lo + HD], NT)

    steps = [(h, b) for h in range(n_heads) for b in range(0, rows, BLK)]
    following = scores(*steps[0])
    for n, (h, b) in enumerate(steps):
        lo = h * HD
        if b == 0:
            v_t = packed_ref[:, width + lo : width + lo + HD].T
        s = following
        if n + 1 < len(steps):
            following = scores(*steps[n + 1])
        s = jnp.where(ks_ref[...] == qs_ref[:, b : b + BLK], s, NEG)
        top = jnp.max(s, axis=0, keepdims=True)
        e = jnp.exp(s - top)
        inv = 1.0 / jnp.sum(e, axis=0, keepdims=True)
        p = (e * inv).astype(BF)
        a_t = dot(v_t, p)
        attn_t[lo : lo + HD, b : b + BLK] = a_t.astype(BF)
        attn_ref[b : b + BLK, lo : lo + HD] = a_t.T.astype(BF)
        top_ref[h : h + 1, b : b + BLK] = top
        inv_ref[h : h + 1, b : b + BLK] = inv
        if h > 0:
            weigh(h - 1, b // BLK)
        if n == rows // BLK - 1:
            for load in cot_loads:
                load.wait()
    attn_store.start()
    for k2 in range(4):
        weigh(n_heads - 1, k2)
        stores[k2].start()
    for store in [packed_store, attn_store] + stores:
        store.wait()


def forward(bounds, secs, cols, rank_row, gathered_kv, queries, ks_col, qs_row, grads):
    rows, width = queries.shape
    kv = ks_col.shape[0]
    part = gathered_kv.shape[1]
    stat = jax.ShapeDtypeStruct((width // HD, rows), F32)
    return pl.pallas_call(
        forward_kernel,
        out_shape=(
            jax.ShapeDtypeStruct((kv, 2 * width), BF),
            jax.ShapeDtypeStruct((rows, width), BF),
            stat, stat,
            jax.ShapeDtypeStruct((4, 4 * width, BLK), BF),
        ),
        in_specs=[SCALARS] * 3 + [WHOLE] + [ANY] * 2 + [WHOLE] * 2 + [ANY] * 8,
        out_specs=(ANY, ANY, WHOLE, WHOLE, ANY),
        scratch_shapes=[
            pltpu.VMEM((4, part, 2 * width), BF),
            pltpu.VMEM((kv, 2 * width), BF),
            pltpu.VMEM((rows, width), BF),
            pltpu.VMEM((rows, width), BF),
            pltpu.VMEM((width, rows), BF),
            pltpu.VMEM((16, rows, BLK), BF),
            pltpu.VMEM((4, 4 * width, BLK), BF),
            DMA((4,)),
            DMA,
            DMA((2,)),
            DMA((16,)),
            DMA((4,)),
        ],
        compiler_params=pltpu.CompilerParams(vmem_limit_bytes=VMEM_BYTES),
        name="gather_forward",
    )(bounds, secs, cols, rank_row, gathered_kv, queries, ks_col, qs_row, *grads)


def backward_kernel(
    bounds, cols, rank_ref, packed_in, q_in, part_in, g0, g1, g2, g3, w_in, ks_ref, qs_ref, top_ref, inv_ref,
    dq_ref, out,
    packed_ref, q_ref, part_ref, cot, w_ref, da_ref, p_f, p_s, ds_s, dp_s, piece, in_sem, g_sem, w_sem, sem,
):
    rows, width = q_ref.shape
    kv = packed_ref.shape[0]
    scale = HD**-0.5
    n_heads = width // HD
    first = [
        pltpu.make_async_copy(packed_in, packed_ref, in_sem.at[0]),
        pltpu.make_async_copy(q_in, q_ref, in_sem.at[1]),
        pltpu.make_async_copy(part_in, part_ref, in_sem.at[2]),
    ]
    later = []
    for n, g in enumerate((g0, g1, g2, g3)):
        later.append(pltpu.make_async_copy(g, cot.at[:, n * width : (n + 1) * width], g_sem.at[n]))
        later.append(
            pltpu.make_async_copy(cut(w_in, cols[n], width), w_ref.at[:, n * width : (n + 1) * width], w_sem.at[n])
        )
    for load in first + later:
        load.start()
    first[0].wait()
    first[1].wait()
    q_ref[...] = q_ref[...] * BF(scale)

    def weights(h, b):
        lo = h * HD
        s = dot(packed_ref[:, lo : lo + HD], q_ref[b : b + BLK, lo : lo + HD], NT)
        s = jnp.where(ks_ref[...] == qs_ref[:, b : b + BLK], s, NEG)
        p = jnp.exp(s - top_ref[h : h + 1, b : b + BLK]) * inv_ref[h : h + 1, b : b + BLK]
        p_f[h, :, b : b + BLK] = p
        p_s[h, :, b : b + BLK] = p.astype(BF)

    for h in range(n_heads):
        for b in range(0, rows, BLK):
            weights(h, b)
    first[2].wait()
    for load in later:
        load.wait()
    for b in range(0, rows, BLK):
        rest = dot(cot[b : b + BLK, :], w_ref[...], NT)
        da_ref[b : b + BLK, :] = (part_ref[b : b + BLK, :] + rest).astype(BF)
    for h in range(n_heads):
        lo = h * HD
        k_t = packed_ref[:, lo : lo + HD].T
        v = packed_ref[:, width + lo : width + lo + HD]
        dp = dot(v, da_ref[0:BLK, lo : lo + HD], NT)
        for b in range(0, rows, BLK):
            following = dot(v, da_ref[b + BLK : b + 2 * BLK, lo : lo + HD], NT) if b + BLK < rows else None
            p = p_f[h, :, b : b + BLK]
            mean = jnp.sum(p * dp, axis=0, keepdims=True)
            ds = (p * (dp - mean)).astype(BF)
            ds_s[h, :, b : b + BLK] = ds
            dq_ref[b : b + BLK, lo : lo + HD] = (dot(k_t, ds) * scale).T.astype(BF)
            dp = following
        dp_s[:, lo : lo + HD] = dot(ds_s[h], q_ref[:, lo : lo + HD]).astype(BF)
        dp_s[:, width + lo : width + lo + HD] = dot(p_s[h], da_ref[:, lo : lo + HD]).astype(BF)
    part = out.shape[1]
    per = part // FINE
    stores = [pltpu.make_async_copy(piece.at[t], out.at[t], sem.at[t]) for t in range(4)]
    for n in range(4):
        for u in range(per):
            t = n * per + u
            start = pl.multiple_of(jnp.minimum(bounds[t] // FINE * FINE, kv - 2 * FINE), FINE)
            at = rank_ref[:, t * FINE : (t + 1) * FINE]
            have = lax.broadcasted_iota(jnp.int32, (2 * FINE, FINE), 0) + start
            put = jnp.where(at == have, 1.0, 0.0).astype(BF)
            piece[n, u * FINE : (u + 1) * FINE, :] = dot(put, dp_s[pl.ds(start, 2 * FINE), :], TN).astype(BF)
        stores[n].start()
    for store in stores:
        store.wait()


def backward(bounds, cols, rank_row, packed, queries, partial, grads, w, ks_col, qs_row, top, inv, part):
    rows, width = queries.shape
    kv = packed.shape[0]
    n_heads = width // HD
    return pl.pallas_call(
        backward_kernel,
        out_shape=(jax.ShapeDtypeStruct((rows, width), BF), jax.ShapeDtypeStruct((4, part, 2 * width), BF)),
        in_specs=[SCALARS] * 2 + [WHOLE] + [ANY] * 8 + [WHOLE] * 4,
        out_specs=(WHOLE, ANY),
        scratch_shapes=[
            pltpu.VMEM((kv, 2 * width), BF),
            pltpu.VMEM((rows, width), BF),
            pltpu.VMEM((rows, width), F32),
            pltpu.VMEM((rows, 4 * width), BF),
            pltpu.VMEM((width, 4 * width), BF),
            pltpu.VMEM((rows, width), BF),
            pltpu.VMEM((n_heads, kv, rows), F32),
            pltpu.VMEM((n_heads, kv, rows), BF),
            pltpu.VMEM((n_heads, kv, rows), BF),
            pltpu.VMEM((kv, 2 * width), BF),
            pltpu.VMEM((4, part, 2 * width), BF),
            DMA((3,)),
            DMA((4,)),
            DMA((4,)),
            DMA((4,)),
        ],
        compiler_params=pltpu.CompilerParams(vmem_limit_bytes=VMEM_BYTES),
        name="backward_scatter",
    )(bounds, cols, rank_row, packed, queries, partial, *grads, w, ks_col, qs_row, top, inv)


def d_attn_kernel(n_blocks, cols, *refs):
    grads, w_in, out_ref = refs[:n_blocks], refs[n_blocks], refs[n_blocks + 1]
    cot, w_ref, g_sem, w_sem = refs[n_blocks + 2 :]
    width = grads[0].shape[1]
    loads = []
    for n, g in enumerate(grads):
        loads.append(pltpu.make_async_copy(g, cot.at[:, n * width : (n + 1) * width], g_sem.at[n]))
        loads.append(
            pltpu.make_async_copy(cut(w_in, cols[n], width), w_ref.at[:, n * width : (n + 1) * width], w_sem.at[n])
        )
    for load in loads:
        load.start()
    for load in loads:
        load.wait()
    for b in range(0, out_ref.shape[0], BLK):
        out_ref[b : b + BLK, :] = dot(cot[b : b + BLK, :], w_ref[...], NT)


def d_attn_partial(cols, grads, w):
    rows, width = grads[0].shape
    heads = w.shape[0]
    n = len(grads)
    return pl.pallas_call(
        functools.partial(d_attn_kernel, n),
        out_shape=jax.ShapeDtypeStruct((rows, heads), F32),
        in_specs=[SCALARS] + [ANY] * (n + 1),
        out_specs=WHOLE,
        scratch_shapes=[
            pltpu.VMEM((rows, n * width), BF),
            pltpu.VMEM((heads, n * width), BF),
            DMA((n,)),
            DMA((n,)),
        ],
        compiler_params=pltpu.CompilerParams(vmem_limit_bytes=VMEM_BYTES),
        name="d_attn_partial",
    )(cols, *grads, w)


def mixed_kernel(n, add, cols, a_in, b_in, w_in, v_in, *refs):
    extra = refs[:add]
    outs = refs[add : add + n]
    a_ref, b_ref, w_ref, v_ref = refs[add + n : add + n + 4]
    bufs = refs[add + n + 4 : add + 2 * n + 4]
    sem, w_sem, v_sem, o_sem = refs[add + 2 * n + 4 :]
    width = w_ref.shape[2]
    blocks = [slice(r, r + BLK) for r in range(0, a_ref.shape[0], BLK)]
    a_loads = [pltpu.make_async_copy(a_in.at[rows, :], a_ref.at[rows, :], sem.at[0, r]) for r, rows in enumerate(blocks)]
    b_loads = [pltpu.make_async_copy(b_in.at[rows, :], b_ref.at[rows, :], sem.at[1, r]) for r, rows in enumerate(blocks)]
    w_loads, v_loads = [], []
    for i in range(n):
        w_loads.append(pltpu.make_async_copy(cut(w_in, cols[2 * i], width), w_ref.at[i], w_sem.at[i]))
        v_loads.append(pltpu.make_async_copy(cut(v_in, cols[2 * i + 1], width), v_ref.at[i], v_sem.at[i]))
    w_loads[0].start()
    v_loads[0].start()
    for a_load, b_load in zip(a_loads, b_loads):
        a_load.start()
        b_load.start()
    for load in w_loads[1:] + v_loads[1:]:
        load.start()
    stores = []
    for i in range(n):
        w_loads[i].wait()
        v_loads[i].wait()
        for r, rows in enumerate(blocks):
            if i == 0:
                a_loads[r].wait()
                b_loads[r].wait()
            got = dot(a_ref[rows, :], w_ref[i]) + dot(b_ref[rows, :], v_ref[i])
            if i < add:
                got = got + extra[i][rows, :].astype(F32)
            bufs[i][rows, :] = got.astype(bufs[i].dtype)
            store = pltpu.make_async_copy(bufs[i].at[rows, :], outs[i].at[rows, :], o_sem.at[i, r])
            store.start()
            stores.append(store)
    for store in stores:
        store.wait()


def mixed_pieces(cols, attn, attn_mate, w, w_mate, kinds, extra=()):
    rows, heads = attn.shape
    width = 512
    n = len(kinds)
    add = len(extra)
    return pl.pallas_call(
        functools.partial(mixed_kernel, n, add),
        out_shape=tuple(jax.ShapeDtypeStruct((rows, width), kind) for kind in kinds),
        in_specs=[SCALARS] + [ANY] * 4 + [WHOLE] * add,
        out_specs=(ANY,) * n,
        scratch_shapes=[
            pltpu.VMEM((rows, heads), BF),
            pltpu.VMEM((rows, heads), BF),
            pltpu.VMEM((n, heads, width), BF),
            pltpu.VMEM((n, heads, width), BF),
        ]
        + [pltpu.VMEM((rows, width), kind) for kind in kinds]
        + [DMA((2, rows // BLK)), DMA((n,)), DMA((n,)), DMA((n, rows // BLK))],
        compiler_params=pltpu.CompilerParams(vmem_limit_bytes=VMEM_BYTES),
        name="mixed_pieces",
    )(cols, attn, attn_mate, w, w_mate, *extra)


def mate_kernel(core, w_in, out_ref, sem):
    width = 512
    copies = [
        pltpu.make_async_copy(cut(w_in, 2 * i + 1 - core[0], width), out_ref.at[:, i * width : (i + 1) * width], sem.at[i])
        for i in range(4)
    ]
    for copy in copies:
        copy.start()
    for copy in copies:
        copy.wait()


def columns_for_mate(core, w):
    heads, cols = w.shape
    return pl.pallas_call(
        mate_kernel,
        out_shape=jax.ShapeDtypeStruct((heads, cols // 2), w.dtype),
        in_specs=[SCALARS, ANY],
        out_specs=WHOLE,
        scratch_shapes=[DMA((4,))],
        compiler_params=pltpu.CompilerParams(vmem_limit_bytes=VMEM_BYTES),
        name="columns_for_mate",
    )(core, w)


def f(v):
    return v.astype(F32)


def after(value, *others):
    return lax.optimization_barrier((value,) + others)[0]


def on_device(queries, keys, values, out_weight, cotangent, pack, kv_seg, q_seg):
    p = lax.axis_index("section").astype(jnp.int32)
    m = lax.axis_index("mp").astype(jnp.int32)
    x, c = m // 2, m % 2
    ahead = 1 - 2 * c
    mem = keys.shape[0]
    width = queries.shape[1]
    first = jnp.where(c == 0, p % 4, p // 4)

    kv = jnp.concatenate((keys, values), axis=1)
    around = [move_first(kv, -k) for k in (1, 2, 3)]
    from_behind = move_ahead(cotangent)

    xs = jnp.stack((x, x, x - ahead, x + ahead, x + ahead, x - ahead, x + 2, x + 2)) % 4
    cols = 2 * xs + jnp.stack((c, 1 - c) * 4)
    d = jnp.arange(16, dtype=jnp.int32)
    to1 = (first + d) % 4
    sections = jnp.where(c == 0, d // 4 * 4 + to1, to1 * 4 + d // 4)

    def pair(to):
        to = to % 4
        return jnp.stack((2 * to + c, to))

    small = (
        sections, cols, cols[4:], pair(x + 2), pair(x + ahead), jnp.concatenate((pair(x - ahead), pair(x))),
    )
    w_send = columns_for_mate(c[None], out_weight)
    *around, from_behind, w_send, small = lax.optimization_barrier((*around, from_behind, w_send, small))
    sections, cols, last_cols, far_cols, ahead_cols, near_cols = small

    near = jnp.concatenate([kv] + around, axis=0)
    gathered_kv = exchange(jnp.broadcast_to(near[None], (4,) + near.shape), SECOND)

    r, near = lax.optimization_barrier((pack[0], near))
    block = r // mem
    a1 = jnp.where(c == 0, block % 4, block // 4)
    a2 = jnp.where(c == 0, block // 4, block % 4)
    idx = (a2 * 4 + (a1 - first) % 4) * mem + r % mem
    rank = jnp.sum((idx[None, :] < idx[:, None]).astype(jnp.int32), axis=1)
    places = jnp.arange(16 * mem, dtype=jnp.int32)
    rank_row = jnp.max(jnp.where(idx[:, None] == places[None, :], rank[:, None], -1), axis=0)[None, :]
    order = jnp.arange(r.shape[0], dtype=jnp.int32)
    seg = jnp.sum(jnp.where(rank[:, None] == order[None, :], kv_seg[0][:, None], 0), axis=0)
    starts = jnp.arange(0, 16 * mem, FINE, dtype=jnp.int32)
    bounds = jnp.sum((idx[None, :] < starts[:, None]).astype(jnp.int32), axis=1)
    ks_col, qs_row = seg[:, None], q_seg[None, :]

    from_far, from_ahead = move_ahead(from_behind), move_behind(after(cotangent, near))
    own_mate = move_core(after(cotangent, near))
    behind_mate = move_core(from_behind)
    grads = (cotangent, own_mate, from_behind, behind_mate)
    partial = d_attn_partial(cols[:4], grads, out_weight)
    bounds, ks_col, rank_row, partial, from_ahead, from_far = lax.optimization_barrier(
        (bounds, ks_col, rank_row, partial, from_ahead, from_far)
    )
    bounds, ahead_mate, far_mate, w_mate = lax.optimization_barrier(
        (bounds, move_core(from_ahead), move_core(from_far), move_core(after(w_send, near)))
    )
    last = (from_ahead, ahead_mate, from_far, far_mate)

    packed, attn, top, inv, pieces = forward(
        bounds, sections, cols, rank_row, gathered_kv, queries, ks_col, qs_row, grads + last
    )
    attn_mate = move_core(attn)
    w_got = exchange(pieces, SECOND)

    (far,) = mixed_pieces(far_cols, attn, attn_mate, out_weight, w_mate, (BF,))
    far_got = move_ahead(far)

    d_queries, d_pieces = backward(
        bounds, last_cols, rank_row, packed, after(queries, far), partial, last, out_weight,
        ks_col, qs_row, top, inv, 4 * mem,
    )
    d_pieces, far_got = lax.optimization_barrier((d_pieces, far_got))
    d_got = exchange(d_pieces, SECOND)

    (to_ahead,) = mixed_pieces(ahead_cols, attn, attn_mate, out_weight, w_mate, (BF,), extra=(far_got,))
    ahead_got = move_ahead(to_ahead)
    to_behind, own = mixed_pieces(near_cols, attn, after(attn_mate, to_ahead), out_weight, w_mate, (BF, F32))
    behind_got = move_behind(to_behind)
    w_got, own = lax.optimization_barrier((w_got, own))

    def added(got):
        return f(got[0]) + f(got[1]) + f(got[2]) + f(got[3])

    def to_send(got, rows):
        return [added([part[k * rows : (k + 1) * rows] for part in got]) for k in range(4)]

    w_own, *w_sums = to_send(w_got, width)
    w_back = [move_first(v.astype(BF), k) for k, v in zip((1, 2, 3), w_sums)]
    d_got, w_back, ahead_got = lax.optimization_barrier((d_got, w_back, ahead_got))
    d_own, *d_sums = to_send(d_got, mem)
    d_back = [move_first(v.astype(BF), k) for k, v in zip((1, 2, 3), d_sums)]
    d_out_weight = added([w_own] + w_back)
    d_keys = added([v[:, :width] for v in [d_own] + d_back])
    d_values = added([v[:, width:] for v in [d_own] + d_back])
    mixed = (own + f(ahead_got) + f(behind_got)).astype(BF)
    return (mixed, d_queries, d_keys, d_values, d_out_weight)


def solution(mesh):
    placed = (
        P("section", "mp"),
        P("section", "mp"),
        P("section", "mp"),
        P("mp", None),
        P("section", "mp"),
        P("section", None),
        P("section", None),
        P("section"),
    )
    return jax.shard_map(
        on_device,
        mesh=mesh,
        in_specs=placed,
        out_specs=(
            P("section", "mp"),
            P("section", "mp"),
            P("section", "mp"),
            P("section", "mp"),
            P("mp", "section"),
        ),
        check_vma=False,
    )
```
